512 devices in a mesh: scen: 64 (over z, y), section: 8 (over x, core).
Axes of the slice: x: 4, y: 4, z: 16, core: 2. Of those that a mesh axis runs over, the one named last changes fastest.
Arguments:
- scen_inverse: bfloat16 [1536, 512, 512], P(('scen', 'section')), as said below
- link_border: bfloat16 [1536, 512, 896], P(('scen', 'section'))
- scen_rhs: bfloat16 [1536, 512], P(('scen', 'section')), may hold values from -0.59765625 to 0.59765625
- link_mask: int32 [1536, 7], P(('scen', 'section')), may hold values 0 or 1
- live_slots: int32 [512], P(('scen', 'section')), may hold values from 1 to 3, as said below
- first_block: float32 [896, 896], P('scen', 'section'), as said below
- first_rhs: float32 [896], replicated, may hold values from -120 to 120
Outputs:
- first_step: float32 [896], replicated
- scen_step: float32 [1536, 512], P(('scen', 'section'))
The draws below stay inside these ranges and needn't reach their ends.
Inputs may be any that keep to these rules, and one draw needn't show every extreme that they name: The first live_slots[d] of device d's 3 slots hold scenarios; some device has all 3 slots live. `scen_inverse`: each scen_inverse_s is symmetric and positive definite. first_block is symmetric with a dominant positive diagonal.
All inputs are finite; a program needn't handle non-finite values. No bound on the sum of `link_mask` on one device may be relied on, other than what follows from the above.
Results may differ from the reference program's by a relative error of at most 0.0024.
Values sent between devices are 32-bit elements; how exact they have to be, the bound alone decides.
No kernel may reach another device: no remote copies, remote signals or barrier semaphores. Data moves between devices by JAX's collectives and lax.ppermute only.
A program may use at most 64 MiB of HBM per device.

```python
import jax
import jax.numpy as jnp
from jax import lax

NS = 512
NL = 896
CAP = 3
SLOTS = 1536
NLB = 7


def draw_scen_inverse(key, part):
    key = jax.random.fold_in(key, 11)
    base_key, diag_key, gain_key = jax.random.split(key, 3)
    base_draw = jax.random.normal(base_key, (NS, NS), jnp.float32)
    diagonal = jax.random.uniform(diag_key, (SLOTS, NS), jnp.float32, 0.5, 2.0)
    gain_row = jax.random.uniform(gain_key, (SLOTS, NS), jnp.float32, 0.7, 1.4)
    shared = jnp.dot(base_draw, base_draw.T, precision=lax.Precision.HIGHEST) / NS
    identity = jnp.eye(NS, dtype=jnp.float32)
    dense_part = gain_row[:, :, None] * shared[None, :, :] * gain_row[:, None, :]
    return (dense_part + diagonal[:, :, None] * identity).astype(jnp.bfloat16)


def draw_first_block(key, part):
    key = jax.random.fold_in(key, 12)
    first_key, second_key = jax.random.split(key)
    random_part = jax.random.uniform(first_key, (NL, NL), jnp.float32, -1.0, 1.0)
    offdiag = (random_part + random_part.T) * (5.0 / NL)
    diagonal = jax.random.uniform(second_key, (NL,), jnp.float32, 10.0, 30.0)
    identity = jnp.eye(NL, dtype=jnp.float32)
    return offdiag * (1.0 - identity) + diagonal[:, None] * identity


def draw_live_slots(key, part):
    key = jax.random.fold_in(key, 13)
    first_key, second_key, third_key = jax.random.split(key, 3)
    devices_count = SLOTS // CAP
    heavy = jax.random.randint(first_key, (devices_count,), 0, 4) == 0
    extra = jnp.minimum(jax.random.randint(second_key, (devices_count,), 1, CAP + 1) + 1, CAP)
    counts = jnp.where(heavy, extra, 1)
    forced = jax.random.randint(third_key, (), 0, devices_count)
    counts = jnp.where(jnp.arange(devices_count) == forced, CAP, counts)
    return counts.astype(jnp.int32)


def draw_link_border(key, part):
    key = jax.random.fold_in(key, 14)
    common_key, random_key, weight_key = jax.random.split(key, 3)
    rising = jnp.sqrt(0.5 + jnp.arange(SLOTS, dtype=jnp.float32) / SLOTS)
    common = jax.random.normal(common_key, (NS, NL), jnp.float32)
    random_part = jax.random.normal(random_key, (SLOTS, NS, NL), jnp.float32)
    roughness = jax.random.uniform(weight_key, (SLOTS,), jnp.float32, 0.8, 1.2)
    border_scale = jnp.sqrt(1000.0 / (SLOTS * NL)) * rising * roughness
    return (border_scale[:, None, None] * (common[None, :, :] + 0.15 * random_part)).astype(jnp.bfloat16)


def place_ends(drawn, rng, smallest, top_value):
    dims = drawn.shape
    index_at = [jax.random.randint(jax.random.fold_in(rng, axis), (), 0, dims[axis]) for axis in range(len(dims))]
    drawn = drawn.at[tuple(index_at)].set(smallest)
    longest = dims.index(max(dims))
    index_at[longest] = (index_at[longest] + 1) % dims[longest]
    return drawn.at[tuple(index_at)].set(top_value)


def level_of(own_key, extent, shards, smallest, top_value):
    loudness = 1.0
    for axis_at, blocks in shards:
        heights = jax.random.uniform(jax.random.fold_in(jax.random.fold_in(own_key, 6), axis_at), (blocks,), jnp.float32, smallest / len(shards), top_value / len(shards))
        loudness = loudness * jnp.repeat(jnp.exp(heights), extent[axis_at] // blocks).reshape((-1,) + (1,) * (len(extent) - 1 - axis_at))
    return loudness


def bell_draw(rng, extent, deviation, limit, pieces=(), held_as=jnp.bfloat16):
    array = jax.random.normal(rng, extent, jnp.float32) * deviation
    if len(pieces) > 0:
        array = level_of(rng, extent, pieces, -0.22, 0.18) * array
    return jnp.clip(array, min=-limit, max=limit).astype(held_as)


def setup_inputs(seed: int = 0) -> dict:
    streams_of = jax.random.split(jax.random.key(seed), 8)
    scen_inverse = draw_scen_inverse(jax.random.fold_in(streams_of[7], 71), 0)
    link_border = draw_link_border(jax.random.fold_in(streams_of[7], 71), 0)
    scen_rhs = bell_draw(streams_of[2], (SLOTS, NS), 0.1, 0.59765625, ((0, 512),))
    link_mask = place_ends((jax.random.randint(streams_of[3], (SLOTS, NLB), 0, 4) < 3).astype(jnp.int32), jax.random.fold_in(streams_of[3], 1), 0, 1)
    live_slots = draw_live_slots(jax.random.fold_in(streams_of[7], 71), 0)
    first_block = draw_first_block(jax.random.fold_in(streams_of[7], 71), 0)
    first_rhs = bell_draw(streams_of[6], (NL,), 20.0, 120.0, (), jnp.float32)
    return {"scen_inverse": scen_inverse, "link_border": link_border, "scen_rhs": scen_rhs, "link_mask": link_mask, "live_slots": live_slots, "first_block": first_block, "first_rhs": first_rhs}


def reference(scen_inverse, link_border, scen_rhs, link_mask, live_slots, first_block, first_rhs):
    slot_ids = jnp.arange(SLOTS, dtype=jnp.int32)
    living = slot_ids % CAP < live_slots[slot_ids // CAP]
    widened = jnp.repeat(link_mask, 128, axis=1).astype(jnp.bfloat16)

    def contribute(carry, entries):
        inverse, raw_border, right, column_mask, is_live = entries
        border = raw_border * column_mask[None, :]
        product = jnp.dot(inverse.astype(jnp.float32), border.astype(jnp.float32), preferred_element_type=jnp.float32).astype(jnp.bfloat16)
        reduced = jnp.dot(inverse.astype(jnp.float32), right.astype(jnp.float32), preferred_element_type=jnp.float32)

        def accumulate(state):
            schur_terms, rhs_terms = state
            schur_terms = schur_terms + jnp.dot(border.T.astype(jnp.float32), product.astype(jnp.float32), preferred_element_type=jnp.float32)
            rhs_terms = rhs_terms + jnp.dot(reduced, border.astype(jnp.float32), precision=lax.Precision.HIGHEST)
            return (schur_terms, rhs_terms)

        def unchanged(state):
            return state
        carry = lax.cond(is_live, accumulate, unchanged, carry)
        return (carry, (product, reduced))
    start = (first_block, jnp.zeros((NL,), jnp.float32))
    (schur_matrix, rhs_terms), (products, reduced_all) = lax.scan(contribute, start, (scen_inverse, link_border, scen_rhs, widened, living))
    rhs_first = first_rhs + rhs_terms
    factor = lax.linalg.cholesky(schur_matrix, symmetrize_input=False)
    forward = lax.linalg.triangular_solve(factor, rhs_first[:, None], left_side=True, lower=True)
    first_step = lax.linalg.triangular_solve(factor, forward, left_side=True, lower=True, transpose_a=True)[:, 0]

    def finish(entries):
        product, reduced, is_live = entries
        moved = jnp.dot(product.astype(jnp.float32), first_step, precision=lax.Precision.HIGHEST)
        return jnp.where(is_live, reduced - moved, jnp.zeros_like(reduced))
    scen_step = lax.map(finish, (products, reduced_all, living))
    return (first_step, scen_step)
```

```python
import functools

import jax
import jax.numpy as jnp
from jax import lax
from jax.experimental import pallas as pl
from jax.experimental.pallas import tpu as pltpu
from jax.sharding import PartitionSpec as P

SIDE = 4
LANES = 128
SUBLANES = 8
F32 = jnp.float32
BF16 = jnp.bfloat16
ROWS_ALONE = (((1,), (1,)), ((), ()))


def halves(value):
    high = value.astype(BF16)
    return high, (value - high.astype(F32)).astype(BF16)


def dot(left, right):
    return jnp.dot(left, right, preferred_element_type=F32)


def dot_rows(left, right):
    return lax.dot_general(left, right, ROWS_ALONE, preferred_element_type=F32)


def mixed(left, right):
    left_high, left_low = halves(left)
    right_high, right_low = halves(right)
    return dot(
        jnp.concatenate([left_high, left_low, left_high], axis=1),
        jnp.concatenate([right_high, right_high, right_low], axis=0),
    )


def mixed_rows(left, right):
    left_high, left_low = halves(left)
    right_high, right_low = halves(right)
    return dot_rows(
        jnp.concatenate([left_high, left_low, left_high], axis=1),
        jnp.concatenate([right_high, right_high, right_low], axis=1),
    )


def panel_base(j, blocks):
    return LANES * (j * blocks - j * (j - 1) // 2)


def terms_kernel(
    blocks, live_ref, place_ref, mask_hbm, inverse_hbm, border_ref, right_hbm, corner_hbm, first_ref,
    keep_ref, send_ref, product_ref, reduced_ref, total_ref, rows_ref, corner_wide_ref, rhs_ref,
    mask_ref, inverse_ref, right_ref, corner_ref, small_sems, inverse_sems,
):
    slot = pl.program_id(0)
    width = blocks * LANES
    corner_rows, corner_cols = corner_ref.shape
    small = [
        pltpu.make_async_copy(source, target, small_sems.at[i])
        for i, (source, target) in enumerate(
            ((mask_hbm, mask_ref), (right_hbm, right_ref), (corner_hbm, corner_ref))
        )
    ]

    def fetch(at):
        return pltpu.make_async_copy(inverse_hbm.at[at], inverse_ref.at[at], inverse_sems.at[at])

    @pl.when(slot == 0)
    def start():
        for at in range(inverse_ref.shape[0]):
            fetch(at).start()
        for copy in small:
            copy.start()
        total_ref[...] = jnp.zeros_like(total_ref)
        corner_wide_ref[...] = jnp.zeros_like(corner_wide_ref)
        for copy in small:
            copy.wait()
        corner_wide_ref[0:corner_rows, 0:corner_cols] = corner_ref[...]
        row_start = place_ref[0] * corner_rows
        col_start = place_ref[1] * corner_cols
        row_base = row_start // SUBLANES * SUBLANES
        col_base = col_start // LANES * LANES
        moved = pltpu.roll(corner_wide_ref[...], col_start - col_base, 1)
        moved = pltpu.roll(moved, row_start - row_base, 0)
        total_ref[
            pl.ds(pl.multiple_of(row_base, SUBLANES), corner_wide_ref.shape[0]),
            pl.ds(pl.multiple_of(col_base, LANES), corner_wide_ref.shape[1]),
        ] = moved
        at_origin = jnp.logical_and(place_ref[0] == 0, place_ref[1] == 0)
        rhs_ref[...] = jnp.where(at_origin, first_ref[...], 0.0)

    fetch(slot).wait()

    @pl.when(slot < live_ref[0])
    def add():
        mask = mask_ref[...]
        mask = jnp.sum(jnp.where(lax.broadcasted_iota(jnp.int32, mask.shape, 0) == slot, mask, 0), axis=0, keepdims=True)
        for c in range(blocks):
            at = slice(c * LANES, (c + 1) * LANES)
            turned = border_ref[0, :, at].T
            rows_ref[at, :] = turned * mask[:, c : c + 1].astype(F32).astype(BF16)
        inverse = inverse_ref[slot]
        product = dot(rows_ref[...], inverse).astype(BF16)
        product_ref[0] = product
        right = right_ref[...].astype(F32)
        right = jnp.sum(jnp.where(lax.broadcasted_iota(jnp.int32, right.shape, 0) == slot, right, 0.0), axis=0, keepdims=True)
        right = jnp.broadcast_to(right, (16, right.shape[1])).astype(BF16)
        reduced = dot(right, inverse)[0:1]
        reduced_ref[0] = reduced
        first, rest = halves(reduced)
        rest_wide = reduced - first.astype(F32)
        second, third = halves(rest_wide)
        row = lax.broadcasted_iota(jnp.int32, (16, reduced.shape[1]), 0)
        pieces = jnp.where(
            row == 0, first.astype(F32), jnp.where(row == 1, second.astype(F32), jnp.where(row == 2, third.astype(F32), 0.0))
        ).astype(BF16)
        rhs_ref[...] += jnp.sum(dot_rows(pieces, rows_ref[...]), axis=0, keepdims=True)
        for c in range(0, width, 2 * LANES):
            end = min(c + 2 * LANES, width)
            total_ref[c:width, c:end] += dot_rows(rows_ref[c:width, :], product[c:end, :])

    @pl.when(slot == pl.num_programs(0) - 1)
    def finish():
        cut = LANES // 2
        right_half = lax.broadcasted_iota(jnp.int32, (1, LANES), 1) >= cut
        places = [(j, i) for j in range(blocks) for i in range(j, blocks)]
        count = len(places) // 2

        def write(out_ref, own_places):
            for at, (j, i) in enumerate(own_places):
                base = at * LANES
                out_ref[base : base + LANES, :] = total_ref[i * LANES : (i + 1) * LANES, j * LANES : (j + 1) * LANES]
                if i == j:
                    own = rhs_ref[:, j * LANES : (j + 1) * LANES]
                    for row, value in ((0, own), (cut - 1, pltpu.roll(own, cut, 1))):
                        line = slice(base + row, base + row + 1)
                        out_ref[line, :] = jnp.where(right_half, value, out_ref[line, :])

        for core in range(2):

            @pl.when(lax.rem(place_ref[1], 2) == core)
            def write_both():
                write(keep_ref, places[core * count : (core + 1) * count])
                write(send_ref, places[(1 - core) * count : (2 - core) * count])


def invert(rows):
    count = len(rows)
    lane = lax.broadcasted_iota(jnp.int32, (SUBLANES, LANES), 1)
    sublane = lax.broadcasted_iota(jnp.int32, (SUBLANES, LANES), 0)
    shape = (SUBLANES, LANES)

    def across(block, c):
        return jnp.broadcast_to(block[:, c : c + 1], shape)

    def down(block, k):
        return jnp.broadcast_to(block[k : k + 1, :], shape)

    for p in range(count):
        at = p * SUBLANES
        own = rows[p]
        columns = [across(own, at + k) for k in range(SUBLANES)]
        inside = jnp.logical_and(lane >= at, lane < at + SUBLANES)
        own = jnp.where(inside, jnp.where(lane - at == sublane, 1.0, 0.0), own)
        scale = jnp.zeros(shape, F32)
        for k in range(SUBLANES):
            pivot = down(columns[k], k)
            inverse = 1.0 / pivot
            factor = jnp.where(sublane == k, 0.0, columns[k]) * inverse
            scale = jnp.where(sublane == k, inverse, scale)
            for m in range(k + 1, SUBLANES):
                columns[m] = columns[m] - factor * down(columns[m], k)
            own = own - factor * down(own, k)
        own = own * scale
        spread = [down(own, k) for k in range(SUBLANES)]
        order = [(p + step) % count for step in range(1, count)]
        for v in order:
            block = rows[v]
            terms = [across(block, at + k) * spread[k] for k in range(SUBLANES)]
            while len(terms) > 1:
                terms = [a + b for a, b in zip(terms[0::2], terms[1::2])]
            rows[v] = jnp.where(inside, 0.0, block) - terms[0]
        rows[p] = own
    return rows


def add_up(parts):
    total = parts[0]
    for i in range(1, parts.shape[0]):
        total = total + parts[i]
    return total


def scatter_sum(value, axis, groups):
    size = len(groups[0])
    parts = value.reshape(size, value.shape[0] // size, LANES)
    return add_up(lax.all_to_all(parts, axis, 0, 0, axis_index_groups=groups))


def exchange(value, axis, groups):
    parts = jnp.broadcast_to(value[None], (len(groups[0]),) + value.shape)
    return lax.all_to_all(parts, axis, 0, 0, axis_index_groups=groups)


def gather(value, axis, groups):
    return exchange(value, axis, groups).reshape(len(groups[0]) * value.shape[0], LANES)


def sum_over_devices(keep, send):
    scen, section = lax.axis_size("scen"), lax.axis_size("section")
    depth = scen // SIDE
    far = depth // SIDE
    both = ("scen", "section")

    def at(z, y, x, core):
        return (z * SIDE + y) * section + 2 * x + core

    cores = [[2 * i, 2 * i + 1] for i in range(SIDE)]
    side = range(SIDE)
    xs, ys = (
        [[[at(z, i, k, core) if along_y else at(z, k, i, core) for i in side] for z in range(depth) for k in side]
        for core in range(2)]
        for along_y in (False, True)
    )
    first, second = xs[0] + ys[1], ys[0] + xs[1]
    near_zs = [[(z * SIDE + i) * SIDE + y for i in side] for z in range(far) for y in side]
    far_zs = [[(i * SIDE + z) * SIDE + y for i in range(far)] for z in side for y in side]
    value = keep + lax.ppermute(send, "section", [(i, i ^ 1) for i in range(section)])
    value = scatter_sum(value, both, first)
    value = scatter_sum(value, both, second)
    value = scatter_sum(value, "scen", near_zs)
    value = add_up(exchange(value, "scen", far_zs))
    value = gather(value, "scen", near_zs)
    value = gather(value, both, second)
    value = gather(value, both, first)
    return gather(value, "section", cores)


def solve_kernel(blocks, packed_ref, step_ref, work_ref, inverse_ref, turned_ref, rhs_ref, z_ref, x_ref):
    lower = lax.broadcasted_iota(jnp.int32, (LANES, LANES), 0) >= lax.broadcasted_iota(jnp.int32, (LANES, LANES), 1)
    half = LANES // 2
    left_half = lax.broadcasted_iota(jnp.int32, (1, LANES), 1) < half
    work_ref[...] = packed_ref[...]
    for j in range(blocks):
        base = panel_base(j, blocks)
        square = work_ref[base : base + LANES, :]
        work_ref[base : base + LANES, :] = jnp.where(lower, square, square.T)
        moved = pltpu.roll(square[half - 1 : half, :], half, 1)
        own = jnp.where(left_half, moved, square[0:1, :])
        rhs_ref[j] = jnp.broadcast_to(own, (SUBLANES, LANES))

    def step(j, carry):
        base = pl.multiple_of(LANES * (j * blocks - lax.div(j * (j - 1), 2)), LANES)
        square = work_ref[pl.ds(base, LANES), :]
        rows = invert([square[v * SUBLANES : (v + 1) * SUBLANES] for v in range(LANES // SUBLANES)])
        inverse_ref[...] = jnp.concatenate(rows, axis=0)
        for jj in range(blocks):

            @pl.when(j == jj)
            def update():
                inverse = inverse_ref[...]
                at = panel_base(jj, blocks)
                rest = blocks - 1 - jj
                z = mixed(rhs_ref[jj], inverse)
                z_ref[jj] = z
                if rest == 0:
                    return
                panel = work_ref[at + LANES : at + (rest + 1) * LANES, :]
                turned = mixed(panel, inverse)
                turned_ref[at + LANES : at + (rest + 1) * LANES, :] = turned
                for s in range(rest):
                    left = jnp.concatenate([turned[s * LANES :, :], z], axis=0)
                    change = mixed_rows(left, panel[s * LANES : (s + 1) * LANES, :])
                    height = (rest - s) * LANES
                    target = panel_base(jj + 1 + s, blocks)
                    work_ref[target : target + height, :] -= change[:height]
                    rhs_ref[jj + 1 + s] -= change[height:]

        return carry

    lax.fori_loop(0, blocks, step, 0)
    for j in reversed(range(blocks)):
        at = panel_base(j, blocks)
        rest = blocks - 1 - j
        x = z_ref[j]
        if rest:
            x = x - mixed(x_ref[:, (j + 1) * LANES :], turned_ref[at + LANES : at + (rest + 1) * LANES, :])
        x_ref[:, j * LANES : (j + 1) * LANES] = x
    step_ref[...] = x_ref[...]


def finish_kernel(live_ref, step_ref, product_ref, reduced_ref, out_ref):
    slot = pl.program_id(0)
    first = step_ref[0:1, :]
    high, rest = halves(first)
    middle, low = halves(first - high.astype(F32))
    row = lax.broadcasted_iota(jnp.int32, (16, first.shape[1]), 0)
    pieces = jnp.where(
        row == 0, high.astype(F32), jnp.where(row == 1, middle.astype(F32), jnp.where(row == 2, low.astype(F32), 0.0))
    ).astype(BF16)
    moved = jnp.sum(dot(pieces, product_ref[0]), axis=0, keepdims=True)
    out_ref[0] = jnp.where(slot < live_ref[0], reduced_ref[0] - moved, 0.0)


def local(scen_inverse, link_border, scen_rhs, link_mask, live_slots, first_block, first_rhs):
    capacity, scen_width, link_width = link_border.shape
    blocks = link_width // LANES
    packed_rows = panel_base(blocks, blocks)
    place = jnp.stack([lax.axis_index("scen"), lax.axis_index("section")]).astype(jnp.int32)
    smem = pl.BlockSpec(memory_space=pltpu.SMEM)
    hbm = pl.BlockSpec(memory_space=pltpu.HBM)

    def in_hbm(value):
        return pltpu.with_memory_space_constraint(value, pltpu.HBM)

    def per_slot(*dims):
        return pl.BlockSpec((1,) + dims, lambda s: (s,) + (0,) * len(dims))

    def whole(*dims):
        return pl.BlockSpec(dims, lambda s: (0,) * len(dims))

    corner_height = -(-(first_block.shape[0] + SUBLANES - 1) // SUBLANES) * SUBLANES
    keep, send, product, reduced = pl.pallas_call(
        functools.partial(terms_kernel, blocks),
        grid=(capacity,),
        in_specs=[
            smem, smem, hbm, hbm,
            per_slot(scen_width, link_width),
            hbm, hbm,
            whole(1, link_width),
        ],
        out_specs=[
            whole(packed_rows // 2, LANES),
            whole(packed_rows // 2, LANES),
            per_slot(link_width, scen_width),
            per_slot(1, scen_width),
        ],
        out_shape=[
            jax.ShapeDtypeStruct((packed_rows // 2, LANES), F32),
            jax.ShapeDtypeStruct((packed_rows // 2, LANES), F32),
            jax.ShapeDtypeStruct((capacity, link_width, scen_width), BF16),
            jax.ShapeDtypeStruct((capacity, 1, scen_width), F32),
        ],
        scratch_shapes=[
            pltpu.VMEM((link_width + 2 * SUBLANES, link_width + LANES), F32),
            pltpu.VMEM((link_width, scen_width), BF16),
            pltpu.VMEM((corner_height, 2 * LANES), F32),
            pltpu.VMEM((1, link_width), F32),
            pltpu.VMEM(link_mask.shape, jnp.int32),
            pltpu.VMEM(scen_inverse.shape, BF16),
            pltpu.VMEM(scen_rhs.shape, BF16),
            pltpu.VMEM(first_block.shape, F32),
            pltpu.SemaphoreType.DMA((3,)),
            pltpu.SemaphoreType.DMA((capacity,)),
        ],
        compiler_params=pltpu.CompilerParams(vmem_limit_bytes=48 * 1024 * 1024),
        name="schur_terms",
    )(
        live_slots, place, in_hbm(link_mask), in_hbm(scen_inverse), link_border, in_hbm(scen_rhs), in_hbm(first_block),
        first_rhs[None, :],
    )
    packed = sum_over_devices(keep, send)
    square = (LANES, LANES)
    step = pl.pallas_call(
        functools.partial(solve_kernel, blocks),
        out_shape=jax.ShapeDtypeStruct((SUBLANES, link_width), F32),
        scratch_shapes=[
            pltpu.VMEM((packed_rows, LANES), F32),
            pltpu.VMEM(square, F32),
            pltpu.VMEM((packed_rows, LANES), F32),
            pltpu.VMEM((blocks, SUBLANES, LANES), F32),
            pltpu.VMEM((blocks, SUBLANES, LANES), F32),
            pltpu.VMEM((SUBLANES, link_width), F32),
        ],
        compiler_params=pltpu.CompilerParams(vmem_limit_bytes=48 * 1024 * 1024),
        name="first_solve",
    )(packed)
    scen_step = pl.pallas_call(
        finish_kernel,
        grid=(capacity,),
        in_specs=[smem, whole(SUBLANES, link_width), per_slot(link_width, scen_width), per_slot(1, scen_width)],
        out_specs=per_slot(1, scen_width),
        out_shape=jax.ShapeDtypeStruct((capacity, 1, scen_width), F32),
        compiler_params=pltpu.CompilerParams(vmem_limit_bytes=48 * 1024 * 1024),
        name="scen_steps",
    )(live_slots, step, product, reduced)
    return step[0], scen_step[:, 0, :]


def solution(mesh):
    return jax.shard_map(
        local,
        mesh=mesh,
        in_specs=(
            P(("scen", "section"), None, None),
            P(("scen", "section"), None, None),
            P(("scen", "section"), None),
            P(("scen", "section"), None),
            P(("scen", "section")),
            P("scen", "section"),
            P(),
        ),
        out_specs=(P(), P(("scen", "section"), None)),
        check_vma=False,
    )
```

```python
import functools

import jax
import jax.numpy as jnp
from jax import lax
from jax.experimental import pallas as pl
from jax.experimental.pallas import tpu as pltpu
from jax.sharding import PartitionSpec as P

SIDE = 4
STRIP = 4
LANES = 128
SUBLANES = 8
F32 = jnp.float32
BF16 = jnp.bfloat16
ROWS_ALONE = (((1,), (1,)), ((), ()))


def halves(value):
    high = value.astype(BF16)
    return high, (value - high.astype(F32)).astype(BF16)


def dot(left, right):
    return jnp.dot(left, right, preferred_element_type=F32)


def dot_rows(left, right):
    return lax.dot_general(left, right, ROWS_ALONE, preferred_element_type=F32)


def mixed(left, right):
    left_high, left_low = halves(left)
    right_high, right_low = halves(right)
    return dot(
        jnp.concatenate([left_high, left_low, left_high], axis=1),
        jnp.concatenate([right_high, right_high, right_low], axis=0),
    )


def mixed_rows(left, right):
    left_high, left_low = halves(left)
    right_high, right_low = halves(right)
    return dot_rows(
        jnp.concatenate([left_high, left_low, left_high], axis=1),
        jnp.concatenate([right_high, right_high, right_low], axis=1),
    )


def panel_base(j, blocks):
    return LANES * (j * blocks - j * (j - 1) // 2)


def terms_kernel(
    blocks, live_ref, place_ref, mask_hbm, inverse_hbm, border_ref, right_hbm, corner_hbm, first_ref,
    keep_ref, send_ref, product_ref, reduced_ref, total_ref, rows_ref, corner_wide_ref, rhs_ref,
    mask_ref, inverse_ref, right_ref, corner_ref, small_sems, inverse_sems,
):
    slot = pl.program_id(0)
    width = blocks * LANES
    corner_rows, corner_cols = corner_ref.shape
    small = [
        pltpu.make_async_copy(source, target, small_sems.at[i])
        for i, (source, target) in enumerate(
            ((mask_hbm, mask_ref), (right_hbm, right_ref), (corner_hbm, corner_ref))
        )
    ]

    def fetch(at):
        return pltpu.make_async_copy(inverse_hbm.at[at], inverse_ref.at[at], inverse_sems.at[at])

    @pl.when(slot == 0)
    def start():
        for at in range(inverse_ref.shape[0]):
            fetch(at).start()
        for copy in small:
            copy.start()
        total_ref[...] = jnp.zeros_like(total_ref)
        corner_wide_ref[...] = jnp.zeros_like(corner_wide_ref)
        for copy in small:
            copy.wait()
        corner_wide_ref[0:corner_rows, 0:corner_cols] = corner_ref[...]
        row_start = place_ref[0] * corner_rows
        col_start = place_ref[1] * corner_cols
        row_base = row_start // SUBLANES * SUBLANES
        col_base = col_start // LANES * LANES
        moved = pltpu.roll(corner_wide_ref[...], col_start - col_base, 1)
        moved = pltpu.roll(moved, row_start - row_base, 0)
        total_ref[
            pl.ds(pl.multiple_of(row_base, SUBLANES), corner_wide_ref.shape[0]),
            pl.ds(pl.multiple_of(col_base, LANES), corner_wide_ref.shape[1]),
        ] = moved
        at_origin = jnp.logical_and(place_ref[0] == 0, place_ref[1] == 0)
        rhs_ref[...] = jnp.where(at_origin, first_ref[...], 0.0)

    fetch(slot).wait()

    @pl.when(slot < live_ref[0])
    def add():
        mask = mask_ref[...]
        mask = jnp.sum(jnp.where(lax.broadcasted_iota(jnp.int32, mask.shape, 0) == slot, mask, 0), axis=0, keepdims=True)
        for c in range(blocks):
            at = slice(c * LANES, (c + 1) * LANES)
            turned = border_ref[0, :, at].T
            rows_ref[at, :] = turned * mask[:, c : c + 1].astype(F32).astype(BF16)
        inverse = inverse_ref[slot]
        product = dot(rows_ref[...], inverse).astype(BF16)
        product_ref[0] = product
        right = right_ref[...].astype(F32)
        right = jnp.sum(jnp.where(lax.broadcasted_iota(jnp.int32, right.shape, 0) == slot, right, 0.0), axis=0, keepdims=True)
        right = jnp.broadcast_to(right, (16, right.shape[1])).astype(BF16)
        reduced = dot(right, inverse)[0:1]
        reduced_ref[0] = reduced
        first, rest = halves(reduced)
        rest_wide = reduced - first.astype(F32)
        second, third = halves(rest_wide)
        row = lax.broadcasted_iota(jnp.int32, (16, reduced.shape[1]), 0)
        pieces = jnp.where(
            row == 0, first.astype(F32), jnp.where(row == 1, second.astype(F32), jnp.where(row == 2, third.astype(F32), 0.0))
        ).astype(BF16)
        rhs_ref[...] += jnp.sum(dot_rows(pieces, rows_ref[...]), axis=0, keepdims=True)
        for c in range(0, width, 2 * LANES):
            end = min(c + 2 * LANES, width)
            total_ref[c:width, c:end] += dot_rows(rows_ref[c:width, :], product[c:end, :])

    @pl.when(slot == pl.num_programs(0) - 1)
    def finish():
        cut = LANES // 2
        right_half = lax.broadcasted_iota(jnp.int32, (1, LANES), 1) >= cut
        places = [(j, i) for j in range(blocks) for i in range(j, blocks)]
        count = len(places) // 2

        def write(out_ref, own_places):
            for at, (j, i) in enumerate(own_places):
                base = at * LANES
                out_ref[base : base + LANES, :] = total_ref[i * LANES : (i + 1) * LANES, j * LANES : (j + 1) * LANES]
                if i == j:
                    own = rhs_ref[:, j * LANES : (j + 1) * LANES]
                    for row, value in ((0, own), (cut - 1, pltpu.roll(own, cut, 1))):
                        line = slice(base + row, base + row + 1)
                        out_ref[line, :] = jnp.where(right_half, value, out_ref[line, :])

        for core in range(2):

            @pl.when(lax.rem(place_ref[1], 2) == core)
            def write_both():
                write(keep_ref, places[core * count : (core + 1) * count])
                write(send_ref, places[(1 - core) * count : (2 - core) * count])


def invert(rows):
    count = len(rows)
    shape = (SUBLANES, LANES)
    lane = lax.broadcasted_iota(jnp.int32, shape, 1)
    sublane = lax.broadcasted_iota(jnp.int32, shape, 0)

    def across(block, c):
        return jnp.broadcast_to(block[:, c : c + 1], shape)

    def down(block, k):
        return jnp.broadcast_to(block[k : k + 1, :], shape)

    for p in range(count):
        at = p * SUBLANES
        strip = range(p // STRIP * STRIP, (p // STRIP + 1) * STRIP)
        carried = p + 1 in strip
        if p == strip[0]:
            own_columns = [across(rows[p], at + k) for k in range(SUBLANES)]
        inside = jnp.logical_and(lane >= at, lane < at + SUBLANES)
        own = jnp.where(inside, jnp.where(lane - at == sublane, 1.0, 0.0), rows[p])
        columns = [own_columns]
        following = []
        if carried:
            following = [across(rows[p + 1], at + k) for k in range(SUBLANES)]
            columns[0] = columns[0] + [across(rows[p], at + SUBLANES + k) for k in range(SUBLANES)]
            columns.append(following + [across(rows[p + 1], at + SUBLANES + k) for k in range(SUBLANES)])
        same = jnp.zeros(shape, F32)
        cross = jnp.zeros(shape, F32)
        for k in range(0, SUBLANES, 2):
            one, two = columns[0][k], columns[0][k + 1]
            a, b, c = down(one, k), down(two, k), down(two, k + 1)
            det = a * c - b * b
            rough = pl.reciprocal(det, approx=True)
            mend = 2.0 - det * rough
            free = jnp.logical_or(sublane < k, sublane > k + 1)
            factors = []
            for half, group in enumerate(columns):
                u, v = group[k], group[k + 1]
                first, second = ((u * c - v * b) * rough) * mend, ((v * a - u * b) * rough) * mend
                if half == 0:
                    first, second = jnp.where(free, first, 0.0), jnp.where(free, second, 0.0)
                factors.append((first, second))
            for m in range(k + 2, len(columns[0])):
                top, bottom = down(columns[0][m], k), down(columns[0][m], k + 1)
                for group, (first, second) in zip(columns, factors):
                    group[m] = (group[m] - first * top) - second * bottom
            first, second = factors[0]
            own = (own - first * down(own, k)) - second * down(own, k + 1)
            inverse = rough * mend
            same = jnp.where(sublane == k, c * inverse, jnp.where(sublane == k + 1, a * inverse, same))
            cross = jnp.where(free, cross, b * inverse)
        above, below = pltpu.roll(own, 1, 0), pltpu.roll(own, SUBLANES - 1, 0)
        own = same * own - cross * jnp.where(lax.rem(sublane, 2) == 0, below, above)
        spread = [down(own, k) for k in range(SUBLANES)]
        for v in [*range(p + 1, strip[-1] + 1), *range(strip[0], p)]:
            block = rows[v]
            spans = following if v == p + 1 else [across(block, at + k) for k in range(SUBLANES)]
            terms = [spans[k] * spread[k] for k in range(SUBLANES)]
            while len(terms) > 1:
                terms = [x + y for x, y in zip(terms[0::2], terms[1::2])]
            rows[v] = jnp.where(inside, 0.0, block) - terms[0]
        rows[p] = own
        if carried:
            own_columns = columns[1][SUBLANES:]
            continue
        others = [v % count for v in range(p + 1, p + 1 + count - STRIP)]
        rest = jnp.concatenate([rows[v] for v in others], axis=0)
        lane_wide = lax.broadcasted_iota(jnp.int32, rest.shape, 1)
        inside = jnp.logical_and(lane_wide >= strip[0] * SUBLANES, lane_wide < (p + 1) * SUBLANES)
        blank = jnp.zeros(shape, F32)
        own_rows = jnp.concatenate([rows[v] if v in strip else blank for v in range(count)], axis=0)
        rest = jnp.where(inside, 0.0, rest) - mixed(jnp.where(inside, rest, 0.0), own_rows)
        for i, v in enumerate(others):
            rows[v] = rest[i * SUBLANES : (i + 1) * SUBLANES]
    return rows


def add_up(parts):
    total = parts[0]
    for i in range(1, parts.shape[0]):
        total = total + parts[i]
    return total


def scatter_sum(value, axis, groups):
    size = len(groups[0])
    parts = value.reshape(size, value.shape[0] // size, LANES)
    return add_up(lax.all_to_all(parts, axis, 0, 0, axis_index_groups=groups))


def exchange(value, axis, groups):
    parts = jnp.broadcast_to(value[None], (len(groups[0]),) + value.shape)
    return lax.all_to_all(parts, axis, 0, 0, axis_index_groups=groups)


def gather(value, axis, groups):
    return exchange(value, axis, groups).reshape(len(groups[0]) * value.shape[0], LANES)


def sum_over_devices(keep, send):
    scen, section = lax.axis_size("scen"), lax.axis_size("section")
    depth = scen // SIDE
    far = depth // SIDE
    both = ("scen", "section")

    def at(z, y, x, core):
        return (z * SIDE + y) * section + 2 * x + core

    cores = [[2 * i, 2 * i + 1] for i in range(SIDE)]
    side = range(SIDE)
    xs, ys = (
        [[[at(z, i, k, core) if along_y else at(z, k, i, core) for i in side] for z in range(depth) for k in side]
        for core in range(2)]
        for along_y in (False, True)
    )
    first, second = xs[0] + ys[1], ys[0] + xs[1]
    near_zs = [[(z * SIDE + i) * SIDE + y for i in side] for z in range(far) for y in side]
    far_zs = [[(i * SIDE + z) * SIDE + y for i in range(far)] for z in side for y in side]
    value = keep + lax.ppermute(send, "section", [(i, i ^ 1) for i in range(section)])
    value = scatter_sum(value, both, first)
    value = scatter_sum(value, both, second)
    value = scatter_sum(value, "scen", near_zs)
    value = add_up(exchange(value, "scen", far_zs))
    value = gather(value, "scen", near_zs)
    value = gather(value, both, second)
    value = gather(value, both, first)
    return gather(value, "section", cores)


def solve_kernel(blocks, packed_ref, step_ref, work_ref, inverse_ref, turned_ref, rhs_ref, z_ref, x_ref):
    row = lax.broadcasted_iota(jnp.int32, (LANES, LANES), 0)
    column = lax.broadcasted_iota(jnp.int32, (LANES, LANES), 1)
    half = LANES // 2
    left_half = lax.broadcasted_iota(jnp.int32, (1, LANES), 1) < half
    scales, scale_columns = [], []
    for j in range(blocks):
        base = panel_base(j, blocks)
        square = packed_ref[base : base + LANES, :]
        scale = lax.rsqrt(jnp.sum(jnp.where(row == column, square, 0.0), axis=0, keepdims=True))
        scales.append(scale)
        scale_columns.append(jnp.sum(jnp.where(row == column, scale, 0.0), axis=1, keepdims=True))
        moved = pltpu.roll(square[half - 1 : half, :], half, 1)
        own = jnp.where(left_half, moved, square[0:1, :]) * scale
        rhs_ref[j] = jnp.broadcast_to(own, (SUBLANES, LANES))
    for j in range(blocks):
        for i in range(j, blocks):
            base = panel_base(j, blocks) + (i - j) * LANES
            square = packed_ref[base : base + LANES, :] * scale_columns[i] * scales[j]
            if i == j:
                square = jnp.where(row >= column, square, square.T)
            work_ref[base : base + LANES, :] = square

    def step(j, carry):
        base = pl.multiple_of(LANES * (j * blocks - lax.div(j * (j - 1), 2)), LANES)
        square = work_ref[pl.ds(base, LANES), :]
        rows = invert([square[v * SUBLANES : (v + 1) * SUBLANES] for v in range(LANES // SUBLANES)])
        inverse_ref[...] = jnp.concatenate(rows, axis=0)
        for jj in range(blocks):

            @pl.when(j == jj)
            def update():
                inverse = inverse_ref[...]
                at = panel_base(jj, blocks)
                rest = blocks - 1 - jj
                z = mixed(rhs_ref[jj], inverse)
                z_ref[jj] = z
                if rest == 0:
                    return
                panel = work_ref[at + LANES : at + (rest + 1) * LANES, :]
                turned = mixed(panel, inverse)
                turned_ref[at + LANES : at + (rest + 1) * LANES, :] = turned
                for s in range(rest):
                    left = jnp.concatenate([turned[s * LANES :, :], z], axis=0)
                    change = mixed_rows(left, panel[s * LANES : (s + 1) * LANES, :])
                    height = (rest - s) * LANES
                    target = panel_base(jj + 1 + s, blocks)
                    work_ref[target : target + height, :] -= change[:height]
                    rhs_ref[jj + 1 + s] -= change[height:]

        return carry

    lax.fori_loop(0, blocks, step, 0)
    for j in reversed(range(blocks)):
        at = panel_base(j, blocks)
        rest = blocks - 1 - j
        x = z_ref[j]
        if rest:
            x = x - mixed(x_ref[:, (j + 1) * LANES :], turned_ref[at + LANES : at + (rest + 1) * LANES, :])
        x_ref[:, j * LANES : (j + 1) * LANES] = x
    for j in range(blocks):
        at = slice(j * LANES, (j + 1) * LANES)
        step_ref[:, at] = x_ref[:, at] * scales[j]


def first_solve(packed):
    blocks = 0
    while panel_base(blocks, blocks) < packed.shape[0]:
        blocks += 1
    square = (LANES, LANES)
    return pl.pallas_call(
        functools.partial(solve_kernel, blocks),
        out_shape=jax.ShapeDtypeStruct((SUBLANES, blocks * LANES), F32),
        scratch_shapes=[
            pltpu.VMEM((packed.shape[0], LANES), F32),
            pltpu.VMEM(square, F32),
            pltpu.VMEM((packed.shape[0], LANES), F32),
            pltpu.VMEM((blocks, SUBLANES, LANES), F32),
            pltpu.VMEM((blocks, SUBLANES, LANES), F32),
            pltpu.VMEM((SUBLANES, blocks * LANES), F32),
        ],
        compiler_params=pltpu.CompilerParams(vmem_limit_bytes=48 * 1024 * 1024),
        name="first_solve",
    )(packed)


def finish_kernel(live_ref, step_ref, product_ref, reduced_ref, out_ref):
    slot = pl.program_id(0)
    first = step_ref[0:1, :]
    high, rest = halves(first)
    middle, low = halves(first - high.astype(F32))
    row = lax.broadcasted_iota(jnp.int32, (16, first.shape[1]), 0)
    pieces = jnp.where(
        row == 0, high.astype(F32), jnp.where(row == 1, middle.astype(F32), jnp.where(row == 2, low.astype(F32), 0.0))
    ).astype(BF16)
    moved = jnp.sum(dot(pieces, product_ref[0]), axis=0, keepdims=True)
    out_ref[0] = jnp.where(slot < live_ref[0], reduced_ref[0] - moved, 0.0)


def local(scen_inverse, link_border, scen_rhs, link_mask, live_slots, first_block, first_rhs):
    capacity, scen_width, link_width = link_border.shape
    blocks = link_width // LANES
    packed_rows = panel_base(blocks, blocks)
    place = jnp.stack([lax.axis_index("scen"), lax.axis_index("section")]).astype(jnp.int32)
    smem = pl.BlockSpec(memory_space=pltpu.SMEM)
    hbm = pl.BlockSpec(memory_space=pltpu.HBM)

    def in_hbm(value):
        return pltpu.with_memory_space_constraint(value, pltpu.HBM)

    def per_slot(*dims):
        return pl.BlockSpec((1,) + dims, lambda s: (s,) + (0,) * len(dims))

    def whole(*dims):
        return pl.BlockSpec(dims, lambda s: (0,) * len(dims))

    corner_height = -(-(first_block.shape[0] + SUBLANES - 1) // SUBLANES) * SUBLANES
    keep, send, product, reduced = pl.pallas_call(
        functools.partial(terms_kernel, blocks),
        grid=(capacity,),
        in_specs=[
            smem, smem, hbm, hbm,
            per_slot(scen_width, link_width),
            hbm, hbm,
            whole(1, link_width),
        ],
        out_specs=[
            whole(packed_rows // 2, LANES),
            whole(packed_rows // 2, LANES),
            per_slot(link_width, scen_width),
            per_slot(1, scen_width),
        ],
        out_shape=[
            jax.ShapeDtypeStruct((packed_rows // 2, LANES), F32),
            jax.ShapeDtypeStruct((packed_rows // 2, LANES), F32),
            jax.ShapeDtypeStruct((capacity, link_width, scen_width), BF16),
            jax.ShapeDtypeStruct((capacity, 1, scen_width), F32),
        ],
        scratch_shapes=[
            pltpu.VMEM((link_width + 2 * SUBLANES, link_width + LANES), F32),
            pltpu.VMEM((link_width, scen_width), BF16),
            pltpu.VMEM((corner_height, 2 * LANES), F32),
            pltpu.VMEM((1, link_width), F32),
            pltpu.VMEM(link_mask.shape, jnp.int32),
            pltpu.VMEM(scen_inverse.shape, BF16),
            pltpu.VMEM(scen_rhs.shape, BF16),
            pltpu.VMEM(first_block.shape, F32),
            pltpu.SemaphoreType.DMA((3,)),
            pltpu.SemaphoreType.DMA((capacity,)),
        ],
        compiler_params=pltpu.CompilerParams(vmem_limit_bytes=48 * 1024 * 1024),
        name="schur_terms",
    )(
        live_slots, place, in_hbm(link_mask), in_hbm(scen_inverse), link_border, in_hbm(scen_rhs), in_hbm(first_block),
        first_rhs[None, :],
    )
    packed = sum_over_devices(keep, send)
    step = first_solve(packed)
    scen_step = pl.pallas_call(
        finish_kernel,
        grid=(capacity,),
        in_specs=[smem, whole(SUBLANES, link_width), per_slot(link_width, scen_width), per_slot(1, scen_width)],
        out_specs=per_slot(1, scen_width),
        out_shape=jax.ShapeDtypeStruct((capacity, 1, scen_width), F32),
        compiler_params=pltpu.CompilerParams(vmem_limit_bytes=48 * 1024 * 1024),
        name="scen_steps",
    )(live_slots, step, product, reduced)
    return step[0], scen_step[:, 0, :]


def solution(mesh):
    return jax.shard_map(
        local,
        mesh=mesh,
        in_specs=(
            P(("scen", "section"), None, None),
            P(("scen", "section"), None, None),
            P(("scen", "section"), None),
            P(("scen", "section"), None),
            P(("scen", "section")),
            P("scen", "section"),
            P(),
        ),
        out_specs=(P(), P(("scen", "section"), None)),
        check_vma=False,
    )
```

```python
import functools

import jax
import jax.numpy as jnp
from jax import lax
from jax.experimental import pallas as pl
from jax.experimental.pallas import tpu as pltpu
from jax.sharding import PartitionSpec as P

SIDE = 4
STRIP = 4
LANES = 128
SUBLANES = 8
F32 = jnp.float32
BF16 = jnp.bfloat16
ROWS_ALONE = (((1,), (1,)), ((), ()))


def halves(value):
    high = value.astype(BF16)
    return high, (value - high.astype(F32)).astype(BF16)


def dot(left, right):
    return jnp.dot(left, right, preferred_element_type=F32)


def dot_rows(left, right):
    return lax.dot_general(left, right, ROWS_ALONE, preferred_element_type=F32)


def mixed(left, right):
    left_high, left_low = halves(left)
    right_high, right_low = halves(right)
    return dot(
        jnp.concatenate([left_high, left_low, left_high], axis=1),
        jnp.concatenate([right_high, right_high, right_low], axis=0),
    )


def mixed_rows(left, right):
    left_high, left_low = halves(left)
    right_high, right_low = halves(right)
    return dot_rows(
        jnp.concatenate([left_high, left_low, left_high], axis=1),
        jnp.concatenate([right_high, right_high, right_low], axis=1),
    )


def panel_base(j, blocks):
    return LANES * (j * blocks - j * (j - 1) // 2)


def terms_kernel(
    blocks, live_ref, place_ref, mask_hbm, inverse_hbm, border_ref, right_hbm, corner_hbm, first_ref,
    keep_ref, send_ref, product_ref, reduced_ref, total_ref, rows_ref, corner_wide_ref, rhs_ref,
    mask_ref, inverse_ref, right_ref, corner_ref, small_sems, inverse_sems,
):
    slot = pl.program_id(0)
    width = blocks * LANES
    corner_rows, corner_cols = corner_ref.shape
    small = [
        pltpu.make_async_copy(source, target, small_sems.at[i])
        for i, (source, target) in enumerate(
            ((mask_hbm, mask_ref), (right_hbm, right_ref), (corner_hbm, corner_ref))
        )
    ]

    def fetch(at):
        return pltpu.make_async_copy(inverse_hbm.at[at], inverse_ref.at[at], inverse_sems.at[at])

    @pl.when(slot == 0)
    def start():
        for at in range(inverse_ref.shape[0]):
            fetch(at).start()
        for copy in small:
            copy.start()
        total_ref[...] = jnp.zeros_like(total_ref)
        corner_wide_ref[...] = jnp.zeros_like(corner_wide_ref)
        for copy in small:
            copy.wait()
        corner_wide_ref[0:corner_rows, 0:corner_cols] = corner_ref[...]
        row_start = place_ref[0] * corner_rows
        col_start = place_ref[1] * corner_cols
        row_base = row_start // SUBLANES * SUBLANES
        col_base = col_start // LANES * LANES
        moved = pltpu.roll(corner_wide_ref[...], col_start - col_base, 1)
        moved = pltpu.roll(moved, row_start - row_base, 0)
        total_ref[
            pl.ds(pl.multiple_of(row_base, SUBLANES), corner_wide_ref.shape[0]),
            pl.ds(pl.multiple_of(col_base, LANES), corner_wide_ref.shape[1]),
        ] = moved
        at_origin = jnp.logical_and(place_ref[0] == 0, place_ref[1] == 0)
        rhs_ref[...] = jnp.where(at_origin, first_ref[...], 0.0)

    fetch(slot).wait()

    @pl.when(slot < live_ref[0])
    def add():
        mask = mask_ref[...]
        mask = jnp.sum(jnp.where(lax.broadcasted_iota(jnp.int32, mask.shape, 0) == slot, mask, 0), axis=0, keepdims=True)
        for c in range(blocks):
            at = slice(c * LANES, (c + 1) * LANES)
            turned = border_ref[0, :, at].T
            rows_ref[at, :] = turned * mask[:, c : c + 1].astype(F32).astype(BF16)
        inverse = inverse_ref[slot]
        product = dot(rows_ref[...], inverse).astype(BF16)
        product_ref[0] = product
        right = right_ref[...].astype(F32)
        right = jnp.sum(jnp.where(lax.broadcasted_iota(jnp.int32, right.shape, 0) == slot, right, 0.0), axis=0, keepdims=True)
        right = jnp.broadcast_to(right, (16, right.shape[1])).astype(BF16)
        reduced = dot(right, inverse)[0:1]
        reduced_ref[0] = reduced
        first, rest = halves(reduced)
        rest_wide = reduced - first.astype(F32)
        second, third = halves(rest_wide)
        row = lax.broadcasted_iota(jnp.int32, (16, reduced.shape[1]), 0)
        pieces = jnp.where(
            row == 0, first.astype(F32), jnp.where(row == 1, second.astype(F32), jnp.where(row == 2, third.astype(F32), 0.0))
        ).astype(BF16)
        rhs_ref[...] += jnp.sum(dot_rows(pieces, rows_ref[...]), axis=0, keepdims=True)
        for c in range(0, width, 2 * LANES):
            end = min(c + 2 * LANES, width)
            total_ref[c:width, c:end] += dot_rows(rows_ref[c:width, :], product[c:end, :])

    @pl.when(slot == pl.num_programs(0) - 1)
    def finish():
        cut = LANES // 2
        right_half = lax.broadcasted_iota(jnp.int32, (1, LANES), 1) >= cut
        places = [(j, i) for j in range(blocks) for i in range(j, blocks)]
        count = len(places) // 2

        def write(out_ref, own_places):
            for at, (j, i) in enumerate(own_places):
                base = at * LANES
                out_ref[base : base + LANES, :] = total_ref[i * LANES : (i + 1) * LANES, j * LANES : (j + 1) * LANES]
                if i == j:
                    own = rhs_ref[:, j * LANES : (j + 1) * LANES]
                    for row, value in ((0, own), (cut - 1, pltpu.roll(own, cut, 1))):
                        line = slice(base + row, base + row + 1)
                        out_ref[line, :] = jnp.where(right_half, value, out_ref[line, :])

        for core in range(2):

            @pl.when(lax.rem(place_ref[1], 2) == core)
            def write_both():
                write(keep_ref, places[core * count : (core + 1) * count])
                write(send_ref, places[(1 - core) * count : (2 - core) * count])


def invert(rows):
    count = len(rows)
    shape = (SUBLANES, LANES)
    lane = lax.broadcasted_iota(jnp.int32, shape, 1)
    sublane = lax.broadcasted_iota(jnp.int32, shape, 0)

    def across(block, c):
        return jnp.broadcast_to(block[:, c : c + 1], shape)

    def down(block, k):
        return jnp.broadcast_to(block[k : k + 1, :], shape)

    for p in range(count):
        at = p * SUBLANES
        strip = range(p // STRIP * STRIP, (p // STRIP + 1) * STRIP)
        carried = p + 1 in strip
        if p == strip[0]:
            own_columns = [across(rows[p], at + k) for k in range(SUBLANES)]
        inside = jnp.logical_and(lane >= at, lane < at + SUBLANES)
        own = jnp.where(inside, jnp.where(lane - at == sublane, 1.0, 0.0), rows[p])
        columns = [own_columns]
        following = []
        if carried:
            following = [across(rows[p + 1], at + k) for k in range(SUBLANES)]
            columns[0] = columns[0] + [across(rows[p], at + SUBLANES + k) for k in range(SUBLANES)]
            columns.append(following + [across(rows[p + 1], at + SUBLANES + k) for k in range(SUBLANES)])
        same = jnp.zeros(shape, F32)
        cross = jnp.zeros(shape, F32)
        for k in range(0, SUBLANES, 2):
            one, two = columns[0][k], columns[0][k + 1]
            a, b, c = down(one, k), down(two, k), down(two, k + 1)
            det = a * c - b * b
            rough = pl.reciprocal(det, approx=True)
            mend = 2.0 - det * rough
            free = jnp.logical_or(sublane < k, sublane > k + 1)
            factors = []
            for half, group in enumerate(columns):
                u, v = group[k], group[k + 1]
                first, second = ((u * c - v * b) * rough) * mend, ((v * a - u * b) * rough) * mend
                if half == 0:
                    first, second = jnp.where(free, first, 0.0), jnp.where(free, second, 0.0)
                factors.append((first, second))
            for m in range(k + 2, len(columns[0])):
                top, bottom = down(columns[0][m], k), down(columns[0][m], k + 1)
                for group, (first, second) in zip(columns, factors):
                    group[m] = (group[m] - first * top) - second * bottom
            first, second = factors[0]
            own = (own - first * down(own, k)) - second * down(own, k + 1)
            inverse = rough * mend
            same = jnp.where(sublane == k, c * inverse, jnp.where(sublane == k + 1, a * inverse, same))
            cross = jnp.where(free, cross, b * inverse)
        above, below = pltpu.roll(own, 1, 0), pltpu.roll(own, SUBLANES - 1, 0)
        own = same * own - cross * jnp.where(lax.rem(sublane, 2) == 0, below, above)
        spread = [down(own, k) for k in range(SUBLANES)]
        for v in [*range(p + 1, strip[-1] + 1), *range(strip[0], p)]:
            block = rows[v]
            spans = following if v == p + 1 else [across(block, at + k) for k in range(SUBLANES)]
            terms = [spans[k] * spread[k] for k in range(SUBLANES)]
            while len(terms) > 1:
                terms = [x + y for x, y in zip(terms[0::2], terms[1::2])]
            rows[v] = jnp.where(inside, 0.0, block) - terms[0]
        rows[p] = own
        if carried:
            own_columns = columns[1][SUBLANES:]
            continue
        others = [v % count for v in range(p + 1, p + 1 + count - STRIP)]
        rest = jnp.concatenate([rows[v] for v in others], axis=0)
        lane_wide = lax.broadcasted_iota(jnp.int32, rest.shape, 1)
        inside = jnp.logical_and(lane_wide >= strip[0] * SUBLANES, lane_wide < (p + 1) * SUBLANES)
        blank = jnp.zeros(shape, F32)
        own_rows = jnp.concatenate([rows[v] if v in strip else blank for v in range(count)], axis=0)
        rest = jnp.where(inside, 0.0, rest) - mixed(jnp.where(inside, rest, 0.0), own_rows)
        for i, v in enumerate(others):
            rows[v] = rest[i * SUBLANES : (i + 1) * SUBLANES]
    return rows


def add_up(parts):
    total = parts[0]
    for i in range(1, parts.shape[0]):
        total = total + parts[i]
    return total


def scatter_sum(value, axis, groups):
    size = len(groups[0])
    parts = value.reshape(size, value.shape[0] // size, LANES)
    return add_up(lax.all_to_all(parts, axis, 0, 0, axis_index_groups=groups))


def exchange(value, axis, groups):
    parts = jnp.broadcast_to(value[None], (len(groups[0]),) + value.shape)
    return lax.all_to_all(parts, axis, 0, 0, axis_index_groups=groups)


def gather(value, axis, groups):
    return exchange(value, axis, groups).reshape(len(groups[0]) * value.shape[0], LANES)


def sum_over_devices(keep, send):
    scen, section = lax.axis_size("scen"), lax.axis_size("section")
    depth = scen // SIDE
    far = depth // SIDE
    both = ("scen", "section")

    def at(z, y, x, core):
        return (z * SIDE + y) * section + 2 * x + core

    cores = [[2 * i, 2 * i + 1] for i in range(SIDE)]
    side, pair = range(SIDE), range(2)
    first, second = [], []
    for core in range(2):

        def along(z, major, minor, core=core):
            x, y = (major, minor) if core == 0 else (minor, major)
            return at(z, y, x, core)

        first += [
            [along(z, i, 2 * high + low) for i in side for low in pair] for z in range(depth) for high in pair
        ]
        second += [
            [along(z * SIDE + near, i, 2 * high + low) for high in pair for near in side]
            for z in range(far) for i in side for low in pair
        ]
    far_zs = [[(i * SIDE + z) * SIDE + y for i in range(far)] for z in side for y in side]
    value = keep + lax.ppermute(send, "section", [(i, i ^ 1) for i in range(section)])
    value = scatter_sum(value, both, first)
    value = scatter_sum(value, both, second)
    value = add_up(exchange(value, "scen", far_zs))
    value = gather(value, both, second)
    value = gather(value, both, first)
    return gather(value, "section", cores)


def solve_kernel(blocks, packed_ref, step_ref, work_ref, inverse_ref, turned_ref, rhs_ref, z_ref, x_ref):
    row = lax.broadcasted_iota(jnp.int32, (LANES, LANES), 0)
    column = lax.broadcasted_iota(jnp.int32, (LANES, LANES), 1)
    half = LANES // 2
    left_half = lax.broadcasted_iota(jnp.int32, (1, LANES), 1) < half
    scales, scale_columns = [], []
    for j in range(blocks):
        base = panel_base(j, blocks)
        square = packed_ref[base : base + LANES, :]
        scale = lax.rsqrt(jnp.sum(jnp.where(row == column, square, 0.0), axis=0, keepdims=True))
        scales.append(scale)
        scale_columns.append(jnp.sum(jnp.where(row == column, scale, 0.0), axis=1, keepdims=True))
        moved = pltpu.roll(square[half - 1 : half, :], half, 1)
        own = jnp.where(left_half, moved, square[0:1, :]) * scale
        rhs_ref[j] = jnp.broadcast_to(own, (SUBLANES, LANES))
    for j in range(blocks):
        for i in range(j, blocks):
            base = panel_base(j, blocks) + (i - j) * LANES
            square = packed_ref[base : base + LANES, :] * scale_columns[i] * scales[j]
            if i == j:
                square = jnp.where(row >= column, square, square.T)
            work_ref[base : base + LANES, :] = square

    def step(j, carry):
        base = pl.multiple_of(LANES * (j * blocks - lax.div(j * (j - 1), 2)), LANES)
        square = work_ref[pl.ds(base, LANES), :]
        rows = invert([square[v * SUBLANES : (v + 1) * SUBLANES] for v in range(LANES // SUBLANES)])
        inverse_ref[...] = jnp.concatenate(rows, axis=0)
        for jj in range(blocks):

            @pl.when(j == jj)
            def update():
                inverse = inverse_ref[...]
                at = panel_base(jj, blocks)
                rest = blocks - 1 - jj
                z = mixed(rhs_ref[jj], inverse)
                z_ref[jj] = z
                if rest == 0:
                    return
                panel = work_ref[at + LANES : at + (rest + 1) * LANES, :]
                turned = mixed(panel, inverse)
                turned_ref[at + LANES : at + (rest + 1) * LANES, :] = turned
                for s in range(rest):
                    left = jnp.concatenate([turned[s * LANES :, :], z], axis=0)
                    change = mixed_rows(left, panel[s * LANES : (s + 1) * LANES, :])
                    height = (rest - s) * LANES
                    target = panel_base(jj + 1 + s, blocks)
                    work_ref[target : target + height, :] -= change[:height]
                    rhs_ref[jj + 1 + s] -= change[height:]

        return carry

    lax.fori_loop(0, blocks, step, 0)
    for j in reversed(range(blocks)):
        at = panel_base(j, blocks)
        rest = blocks - 1 - j
        x = z_ref[j]
        if rest:
            x = x - mixed(x_ref[:, (j + 1) * LANES :], turned_ref[at + LANES : at + (rest + 1) * LANES, :])
        x_ref[:, j * LANES : (j + 1) * LANES] = x
    for j in range(blocks):
        at = slice(j * LANES, (j + 1) * LANES)
        step_ref[:, at] = x_ref[:, at] * scales[j]


def first_solve(packed):
    blocks = 0
    while panel_base(blocks, blocks) < packed.shape[0]:
        blocks += 1
    square = (LANES, LANES)
    return pl.pallas_call(
        functools.partial(solve_kernel, blocks),
        out_shape=jax.ShapeDtypeStruct((SUBLANES, blocks * LANES), F32),
        scratch_shapes=[
            pltpu.VMEM((packed.shape[0], LANES), F32),
            pltpu.VMEM(square, F32),
            pltpu.VMEM((packed.shape[0], LANES), F32),
            pltpu.VMEM((blocks, SUBLANES, LANES), F32),
            pltpu.VMEM((blocks, SUBLANES, LANES), F32),
            pltpu.VMEM((SUBLANES, blocks * LANES), F32),
        ],
        compiler_params=pltpu.CompilerParams(vmem_limit_bytes=48 * 1024 * 1024),
        name="first_solve",
    )(packed)


def finish_kernel(live_ref, step_ref, product_ref, reduced_ref, out_ref):
    slot = pl.program_id(0)
    first = step_ref[0:1, :]
    high, rest = halves(first)
    middle, low = halves(first - high.astype(F32))
    row = lax.broadcasted_iota(jnp.int32, (16, first.shape[1]), 0)
    pieces = jnp.where(
        row == 0, high.astype(F32), jnp.where(row == 1, middle.astype(F32), jnp.where(row == 2, low.astype(F32), 0.0))
    ).astype(BF16)
    moved = jnp.sum(dot(pieces, product_ref[0]), axis=0, keepdims=True)
    out_ref[0] = jnp.where(slot < live_ref[0], reduced_ref[0] - moved, 0.0)


def local(scen_inverse, link_border, scen_rhs, link_mask, live_slots, first_block, first_rhs):
    capacity, scen_width, link_width = link_border.shape
    blocks = link_width // LANES
    packed_rows = panel_base(blocks, blocks)
    place = jnp.stack([lax.axis_index("scen"), lax.axis_index("section")]).astype(jnp.int32)
    smem = pl.BlockSpec(memory_space=pltpu.SMEM)
    hbm = pl.BlockSpec(memory_space=pltpu.HBM)

    def in_hbm(value):
        return pltpu.with_memory_space_constraint(value, pltpu.HBM)

    def per_slot(*dims):
        return pl.BlockSpec((1,) + dims, lambda s: (s,) + (0,) * len(dims))

    def whole(*dims):
        return pl.BlockSpec(dims, lambda s: (0,) * len(dims))

    corner_height = -(-(first_block.shape[0] + SUBLANES - 1) // SUBLANES) * SUBLANES
    keep, send, product, reduced = pl.pallas_call(
        functools.partial(terms_kernel, blocks),
        grid=(capacity,),
        in_specs=[
            smem, smem, hbm, hbm,
            per_slot(scen_width, link_width),
            hbm, hbm,
            whole(1, link_width),
        ],
        out_specs=[
            whole(packed_rows // 2, LANES),
            whole(packed_rows // 2, LANES),
            per_slot(link_width, scen_width),
            per_slot(1, scen_width),
        ],
        out_shape=[
            jax.ShapeDtypeStruct((packed_rows // 2, LANES), F32),
            jax.ShapeDtypeStruct((packed_rows // 2, LANES), F32),
            jax.ShapeDtypeStruct((capacity, link_width, scen_width), BF16),
            jax.ShapeDtypeStruct((capacity, 1, scen_width), F32),
        ],
        scratch_shapes=[
            pltpu.VMEM((link_width + 2 * SUBLANES, link_width + LANES), F32),
            pltpu.VMEM((link_width, scen_width), BF16),
            pltpu.VMEM((corner_height, 2 * LANES), F32),
            pltpu.VMEM((1, link_width), F32),
            pltpu.VMEM(link_mask.shape, jnp.int32),
            pltpu.VMEM(scen_inverse.shape, BF16),
            pltpu.VMEM(scen_rhs.shape, BF16),
            pltpu.VMEM(first_block.shape, F32),
            pltpu.SemaphoreType.DMA((3,)),
            pltpu.SemaphoreType.DMA((capacity,)),
        ],
        compiler_params=pltpu.CompilerParams(vmem_limit_bytes=48 * 1024 * 1024),
        name="schur_terms",
    )(
        live_slots, place, in_hbm(link_mask), in_hbm(scen_inverse), link_border, in_hbm(scen_rhs), in_hbm(first_block),
        first_rhs[None, :],
    )
    packed = sum_over_devices(keep, send)
    step = first_solve(packed)
    scen_step = pl.pallas_call(
        finish_kernel,
        grid=(capacity,),
        in_specs=[smem, whole(SUBLANES, link_width), per_slot(link_width, scen_width), per_slot(1, scen_width)],
        out_specs=per_slot(1, scen_width),
        out_shape=jax.ShapeDtypeStruct((capacity, 1, scen_width), F32),
        compiler_params=pltpu.CompilerParams(vmem_limit_bytes=48 * 1024 * 1024),
        name="scen_steps",
    )(live_slots, step, product, reduced)
    return step[0], scen_step[:, 0, :]


def solution(mesh):
    return jax.shard_map(
        local,
        mesh=mesh,
        in_specs=(
            P(("scen", "section"), None, None),
            P(("scen", "section"), None, None),
            P(("scen", "section"), None),
            P(("scen", "section"), None),
            P(("scen", "section")),
            P("scen", "section"),
            P(),
        ),
        out_specs=(P(), P(("scen", "section"), None)),
        check_vma=False,
    )
```

```python
import functools

import jax
import jax.numpy as jnp
from jax import lax
from jax.experimental import pallas as pl
from jax.experimental.pallas import tpu as pltpu
from jax.sharding import PartitionSpec as P

SIDE = 4
STRIP = 4
LANES = 128
SUBLANES = 8
F32 = jnp.float32
BF16 = jnp.bfloat16
ROWS_ALONE = (((1,), (1,)), ((), ()))


def halves(value):
    high = value.astype(BF16)
    return high, (value - high.astype(F32)).astype(BF16)


def dot(left, right):
    return jnp.dot(left, right, preferred_element_type=F32)


def dot_rows(left, right):
    return lax.dot_general(left, right, ROWS_ALONE, preferred_element_type=F32)


def mixed(left, right):
    left_high, left_low = halves(left)
    right_high, right_low = halves(right)
    return dot(
        jnp.concatenate([left_high, left_low, left_high], axis=1),
        jnp.concatenate([right_high, right_high, right_low], axis=0),
    )


def mixed_rows(left, right):
    left_high, left_low = halves(left)
    right_high, right_low = halves(right)
    return dot_rows(
        jnp.concatenate([left_high, left_low, left_high], axis=1),
        jnp.concatenate([right_high, right_high, right_low], axis=1),
    )


def panel_base(j, blocks):
    return LANES * (j * blocks - j * (j - 1) // 2)


def terms_kernel(
    blocks, live_ref, place_ref, mask_hbm, inverse_hbm, border_ref, right_hbm, corner_hbm, first_ref,
    keep_ref, send_ref, product_ref, reduced_ref, total_ref, rows_ref, corner_wide_ref, rhs_ref,
    mask_ref, inverse_ref, right_ref, corner_ref, small_sems, inverse_sems,
):
    slot = pl.program_id(0)
    width = blocks * LANES
    corner_rows, corner_cols = corner_ref.shape
    small = [
        pltpu.make_async_copy(source, target, small_sems.at[i])
        for i, (source, target) in enumerate(
            ((mask_hbm, mask_ref), (right_hbm, right_ref), (corner_hbm, corner_ref))
        )
    ]

    def fetch(at):
        return pltpu.make_async_copy(inverse_hbm.at[at], inverse_ref.at[at], inverse_sems.at[at])

    @pl.when(slot == 0)
    def start():
        for at in range(inverse_ref.shape[0]):
            fetch(at).start()
        for copy in small:
            copy.start()
        total_ref[...] = jnp.zeros_like(total_ref)
        corner_wide_ref[...] = jnp.zeros_like(corner_wide_ref)
        for copy in small:
            copy.wait()
        corner_wide_ref[0:corner_rows, 0:corner_cols] = corner_ref[...]
        row_start = place_ref[0] * corner_rows
        col_start = place_ref[1] * corner_cols
        row_base = row_start // SUBLANES * SUBLANES
        col_base = col_start // LANES * LANES
        moved = pltpu.roll(corner_wide_ref[...], col_start - col_base, 1)
        moved = pltpu.roll(moved, row_start - row_base, 0)
        total_ref[
            pl.ds(pl.multiple_of(row_base, SUBLANES), corner_wide_ref.shape[0]),
            pl.ds(pl.multiple_of(col_base, LANES), corner_wide_ref.shape[1]),
        ] = moved
        at_origin = jnp.logical_and(place_ref[0] == 0, place_ref[1] == 0)
        rhs_ref[...] = jnp.where(at_origin, first_ref[...], 0.0)

    fetch(slot).wait()

    @pl.when(slot < live_ref[0])
    def add():
        mask = mask_ref[...]
        mask = jnp.sum(jnp.where(lax.broadcasted_iota(jnp.int32, mask.shape, 0) == slot, mask, 0), axis=0, keepdims=True)
        for c in range(blocks):
            at = slice(c * LANES, (c + 1) * LANES)
            turned = border_ref[0, :, at].T
            rows_ref[at, :] = turned * mask[:, c : c + 1].astype(F32).astype(BF16)
        inverse = inverse_ref[slot]
        product = dot(rows_ref[...], inverse).astype(BF16)
        product_ref[0] = product
        right = right_ref[...].astype(F32)
        right = jnp.sum(jnp.where(lax.broadcasted_iota(jnp.int32, right.shape, 0) == slot, right, 0.0), axis=0, keepdims=True)
        right = jnp.broadcast_to(right, (16, right.shape[1])).astype(BF16)
        reduced = dot(right, inverse)[0:1]
        reduced_ref[0] = reduced
        first, rest = halves(reduced)
        rest_wide = reduced - first.astype(F32)
        second, third = halves(rest_wide)
        row = lax.broadcasted_iota(jnp.int32, (16, reduced.shape[1]), 0)
        pieces = jnp.where(
            row == 0, first.astype(F32), jnp.where(row == 1, second.astype(F32), jnp.where(row == 2, third.astype(F32), 0.0))
        ).astype(BF16)
        rhs_ref[...] += jnp.sum(dot_rows(pieces, rows_ref[...]), axis=0, keepdims=True)
        for c in range(0, width, 2 * LANES):
            end = min(c + 2 * LANES, width)
            total_ref[c:width, c:end] += dot_rows(rows_ref[c:width, :], product[c:end, :])

    @pl.when(slot == pl.num_programs(0) - 1)
    def finish():
        cut = LANES // 2
        right_half = lax.broadcasted_iota(jnp.int32, (1, LANES), 1) >= cut
        places = [(j, i) for j in range(blocks) for i in range(j, blocks)]
        count = len(places) // 2

        def write(out_ref, own_places):
            for at, (j, i) in enumerate(own_places):
                base = at * LANES
                out_ref[base : base + LANES, :] = total_ref[i * LANES : (i + 1) * LANES, j * LANES : (j + 1) * LANES]
                if i == j:
                    own = rhs_ref[:, j * LANES : (j + 1) * LANES]
                    for row, value in ((0, own), (cut - 1, pltpu.roll(own, cut, 1))):
                        line = slice(base + row, base + row + 1)
                        out_ref[line, :] = jnp.where(right_half, value, out_ref[line, :])

        for core in range(2):

            @pl.when(lax.rem(place_ref[1], 2) == core)
            def write_both():
                write(keep_ref, places[core * count : (core + 1) * count])
                write(send_ref, places[(1 - core) * count : (2 - core) * count])


def invert(rows):
    count = len(rows)
    shape = (SUBLANES, LANES)
    lane = lax.broadcasted_iota(jnp.int32, shape, 1)
    sublane = lax.broadcasted_iota(jnp.int32, shape, 0)

    def across(block, c):
        return jnp.broadcast_to(block[:, c : c + 1], shape)

    def down(block, k):
        return jnp.broadcast_to(block[k : k + 1, :], shape)

    for p in range(count):
        at = p * SUBLANES
        strip = range(p // STRIP * STRIP, (p // STRIP + 1) * STRIP)
        carried = p + 1 in strip
        if p == strip[0]:
            own_columns = [across(rows[p], at + k) for k in range(SUBLANES)]
        inside = jnp.logical_and(lane >= at, lane < at + SUBLANES)
        own = jnp.where(inside, jnp.where(lane - at == sublane, 1.0, 0.0), rows[p])
        columns = [own_columns]
        following = []
        if carried:
            following = [across(rows[p + 1], at + k) for k in range(SUBLANES)]
            columns[0] = columns[0] + [across(rows[p], at + SUBLANES + k) for k in range(SUBLANES)]
            columns.append(following + [across(rows[p + 1], at + SUBLANES + k) for k in range(SUBLANES)])
        same = jnp.zeros(shape, F32)
        cross = jnp.zeros(shape, F32)
        for k in range(0, SUBLANES, 2):
            one, two = columns[0][k], columns[0][k + 1]
            a, b, c = down(one, k), down(two, k), down(two, k + 1)
            det = a * c - b * b
            rough = pl.reciprocal(det, approx=True)
            mend = 2.0 - det * rough
            free = jnp.logical_or(sublane < k, sublane > k + 1)
            factors = []
            for half, group in enumerate(columns):
                u, v = group[k], group[k + 1]
                first, second = ((u * c - v * b) * rough) * mend, ((v * a - u * b) * rough) * mend
                if half == 0:
                    first, second = jnp.where(free, first, 0.0), jnp.where(free, second, 0.0)
                factors.append((first, second))
            for m in range(k + 2, len(columns[0])):
                top, bottom = down(columns[0][m], k), down(columns[0][m], k + 1)
                for group, (first, second) in zip(columns, factors):
                    group[m] = (group[m] - first * top) - second * bottom
            first, second = factors[0]
            own = (own - first * down(own, k)) - second * down(own, k + 1)
            inverse = rough * mend
            same = jnp.where(sublane == k, c * inverse, jnp.where(sublane == k + 1, a * inverse, same))
            cross = jnp.where(free, cross, b * inverse)
        above, below = pltpu.roll(own, 1, 0), pltpu.roll(own, SUBLANES - 1, 0)
        own = same * own - cross * jnp.where(lax.rem(sublane, 2) == 0, below, above)
        spread = [down(own, k) for k in range(SUBLANES)]
        for v in [*range(p + 1, strip[-1] + 1), *range(strip[0], p)]:
            block = rows[v]
            spans = following if v == p + 1 else [across(block, at + k) for k in range(SUBLANES)]
            terms = [spans[k] * spread[k] for k in range(SUBLANES)]
            while len(terms) > 1:
                terms = [x + y for x, y in zip(terms[0::2], terms[1::2])]
            rows[v] = jnp.where(inside, 0.0, block) - terms[0]
        rows[p] = own
        if carried:
            own_columns = columns[1][SUBLANES:]
            continue
        others = [v % count for v in range(p + 1, p + 1 + count - STRIP)]
        rest = jnp.concatenate([rows[v] for v in others], axis=0)
        lane_wide = lax.broadcasted_iota(jnp.int32, rest.shape, 1)
        inside = jnp.logical_and(lane_wide >= strip[0] * SUBLANES, lane_wide < (p + 1) * SUBLANES)
        blank = jnp.zeros(shape, F32)
        own_rows = jnp.concatenate([rows[v] if v in strip else blank for v in range(count)], axis=0)
        rest = jnp.where(inside, 0.0, rest) - mixed(jnp.where(inside, rest, 0.0), own_rows)
        for i, v in enumerate(others):
            rows[v] = rest[i * SUBLANES : (i + 1) * SUBLANES]
    return rows


def add_up(parts):
    total = parts[0]
    for i in range(1, parts.shape[0]):
        total = total + parts[i]
    return total


def scatter_sum(value, axis, groups):
    size = len(groups[0])
    parts = value.reshape(size, value.shape[0] // size, LANES)
    return add_up(lax.all_to_all(parts, axis, 0, 0, axis_index_groups=groups))


def exchange(value, axis, groups):
    parts = jnp.broadcast_to(value[None], (len(groups[0]),) + value.shape)
    return lax.all_to_all(parts, axis, 0, 0, axis_index_groups=groups)


def gather(value, axis, groups):
    return exchange(value, axis, groups).reshape(len(groups[0]) * value.shape[0], LANES)


def sum_over_devices(keep, send):
    scen, section = lax.axis_size("scen"), lax.axis_size("section")
    depth = scen // SIDE
    far = depth // SIDE
    both = ("scen", "section")

    def at(z, y, x, core):
        return (z * SIDE + y) * section + 2 * x + core

    side, pair = range(SIDE), range(2)
    first, second = [], []
    for core in range(2):

        def along(z, major, minor, core=core):
            x, y = (major, minor) if core == 0 else (minor, major)
            return at(z, y, x, core)

        first += [
            [along(z, i, 2 * high + low) for i in side for low in pair] for z in range(depth) for high in pair
        ]
        second += [
            [along(z * SIDE + near, i, 2 * high + low) for high in pair for near in side]
            for z in range(far) for i in side for low in pair
        ]
    far_zs = [[(i * SIDE + z) * SIDE + y for i in range(far)] for z in side for y in side]
    value = keep + lax.ppermute(send, "section", [(i, i ^ 1) for i in range(section)])
    value = scatter_sum(value, both, first)
    value = scatter_sum(value, both, second)
    value = add_up(exchange(value, "scen", far_zs))
    value = gather(value, both, second)
    value = gather(value, both, first)
    return value, lax.ppermute(value, "section", [(i, i ^ 1) for i in range(section)])


def solve_kernel(blocks, core_ref, own_ref, other_ref, step_ref, work_ref, inverse_ref, turned_ref, rhs_ref, z_ref, x_ref):
    row = lax.broadcasted_iota(jnp.int32, (LANES, LANES), 0)
    column = lax.broadcasted_iota(jnp.int32, (LANES, LANES), 1)
    half = LANES // 2
    left_half = lax.broadcasted_iota(jnp.int32, (1, LANES), 1) < half
    scales, scale_columns = [], []
    height = own_ref.shape[0]

    def packed(base):
        at = slice(base % height, base % height + LANES)
        return jnp.where(core_ref[0] == base // height, own_ref[at, :], other_ref[at, :])

    for j in range(blocks):
        base = panel_base(j, blocks)
        square = packed(base)
        scale = lax.rsqrt(jnp.sum(jnp.where(row == column, square, 0.0), axis=0, keepdims=True))
        scales.append(scale)
        scale_columns.append(jnp.sum(jnp.where(row == column, scale, 0.0), axis=1, keepdims=True))
        moved = pltpu.roll(square[half - 1 : half, :], half, 1)
        own = jnp.where(left_half, moved, square[0:1, :]) * scale
        rhs_ref[j] = jnp.broadcast_to(own, (SUBLANES, LANES))
    for j in range(blocks):
        for i in range(j, blocks):
            base = panel_base(j, blocks) + (i - j) * LANES
            square = packed(base) * scale_columns[i] * scales[j]
            if i == j:
                square = jnp.where(row >= column, square, square.T)
            work_ref[base : base + LANES, :] = square

    def step(j, carry):
        base = pl.multiple_of(LANES * (j * blocks - lax.div(j * (j - 1), 2)), LANES)
        square = work_ref[pl.ds(base, LANES), :]
        rows = invert([square[v * SUBLANES : (v + 1) * SUBLANES] for v in range(LANES // SUBLANES)])
        inverse_ref[...] = jnp.concatenate(rows, axis=0)
        for jj in range(blocks):

            @pl.when(j == jj)
            def update():
                inverse = inverse_ref[...]
                at = panel_base(jj, blocks)
                rest = blocks - 1 - jj
                z = mixed(rhs_ref[jj], inverse)
                z_ref[jj] = z
                if rest == 0:
                    return
                panel_high, panel_low = halves(work_ref[at + LANES : at + (rest + 1) * LANES, :])
                high, low = halves(inverse)
                turned = dot(
                    jnp.concatenate([panel_high, panel_low, panel_high], axis=1),
                    jnp.concatenate([high, high, low], axis=0),
                )
                turned_ref[at + LANES : at + (rest + 1) * LANES, :] = turned
                high, low = halves(jnp.concatenate([turned, z, z], axis=0))
                left = jnp.concatenate([high, low, high], axis=1)
                right = jnp.concatenate([panel_high, panel_high, panel_low], axis=1)
                for s in range(0, rest, 2):
                    change = dot_rows(left[s * LANES :], right[s * LANES : min(s + 2, rest) * LANES])
                    for t in range(s, min(s + 2, rest)):
                        own = change[(t - s) * LANES :, (t - s) * LANES : (t - s + 1) * LANES]
                        height = (rest - t) * LANES
                        target = panel_base(jj + 1 + t, blocks)
                        work_ref[target : target + height, :] -= own[:height]
                        rhs_ref[jj + 1 + t] -= own[height : height + SUBLANES]

        return carry

    lax.fori_loop(0, blocks, step, 0)
    for j in reversed(range(blocks)):
        at = panel_base(j, blocks)
        rest = blocks - 1 - j
        x = z_ref[j]
        if rest:
            x = x - mixed(x_ref[:, (j + 1) * LANES :], turned_ref[at + LANES : at + (rest + 1) * LANES, :])
        x_ref[:, j * LANES : (j + 1) * LANES] = x
    for j in range(blocks):
        at = slice(j * LANES, (j + 1) * LANES)
        step_ref[:, at] = x_ref[:, at] * scales[j]


def first_solve(blocks, core, own, other):
    rows = panel_base(blocks, blocks)
    vmem = pl.BlockSpec(memory_space=pltpu.VMEM)
    square = (LANES, LANES)
    return pl.pallas_call(
        functools.partial(solve_kernel, blocks),
        in_specs=[pl.BlockSpec(memory_space=pltpu.SMEM), vmem, vmem],
        out_shape=jax.ShapeDtypeStruct((SUBLANES, blocks * LANES), F32),
        scratch_shapes=[
            pltpu.VMEM((rows, LANES), F32),
            pltpu.VMEM(square, F32),
            pltpu.VMEM((rows, LANES), F32),
            pltpu.VMEM((blocks, SUBLANES, LANES), F32),
            pltpu.VMEM((blocks, SUBLANES, LANES), F32),
            pltpu.VMEM((SUBLANES, blocks * LANES), F32),
        ],
        compiler_params=pltpu.CompilerParams(vmem_limit_bytes=48 * 1024 * 1024),
        name="first_solve",
    )(core, own, other)


def finish_kernel(live_ref, step_ref, product_ref, reduced_ref, first_ref, out_ref):
    slot = pl.program_id(0)
    first = step_ref[0:1, :]
    high, rest = halves(first)
    middle, low = halves(first - high.astype(F32))
    row = lax.broadcasted_iota(jnp.int32, (16, first.shape[1]), 0)
    pieces = jnp.where(
        row == 0, high.astype(F32), jnp.where(row == 1, middle.astype(F32), jnp.where(row == 2, low.astype(F32), 0.0))
    ).astype(BF16)
    moved = jnp.sum(dot(pieces, product_ref[0]), axis=0, keepdims=True)
    out_ref[pl.ds(slot, 1), :] = jnp.where(slot < live_ref[0], reduced_ref[0] - moved, 0.0)
    first_ref[...] = first[0]


def local(scen_inverse, link_border, scen_rhs, link_mask, live_slots, first_block, first_rhs):
    capacity, scen_width, link_width = link_border.shape
    blocks = link_width // LANES
    packed_rows = panel_base(blocks, blocks)
    place = jnp.stack([lax.axis_index("scen"), lax.axis_index("section")]).astype(jnp.int32)
    smem = pl.BlockSpec(memory_space=pltpu.SMEM)
    hbm = pl.BlockSpec(memory_space=pltpu.HBM)

    def in_hbm(value):
        return pltpu.with_memory_space_constraint(value, pltpu.HBM)

    def per_slot(*dims):
        return pl.BlockSpec((1,) + dims, lambda s: (s,) + (0,) * len(dims))

    def whole(*dims):
        return pl.BlockSpec(dims, lambda s: (0,) * len(dims))

    corner_height = -(-(first_block.shape[0] + SUBLANES - 1) // SUBLANES) * SUBLANES
    keep, send, product, reduced = pl.pallas_call(
        functools.partial(terms_kernel, blocks),
        grid=(capacity,),
        in_specs=[
            smem, smem, hbm, hbm,
            per_slot(scen_width, link_width),
            hbm, hbm,
            whole(1, link_width),
        ],
        out_specs=[
            whole(packed_rows // 2, LANES),
            whole(packed_rows // 2, LANES),
            per_slot(link_width, scen_width),
            per_slot(1, scen_width),
        ],
        out_shape=[
            jax.ShapeDtypeStruct((packed_rows // 2, LANES), F32),
            jax.ShapeDtypeStruct((packed_rows // 2, LANES), F32),
            jax.ShapeDtypeStruct((capacity, link_width, scen_width), BF16),
            jax.ShapeDtypeStruct((capacity, 1, scen_width), F32),
        ],
        scratch_shapes=[
            pltpu.VMEM((link_width + 2 * SUBLANES, link_width + LANES), F32),
            pltpu.VMEM((link_width, scen_width), BF16),
            pltpu.VMEM((corner_height, 2 * LANES), F32),
            pltpu.VMEM((1, link_width), F32),
            pltpu.VMEM(link_mask.shape, jnp.int32),
            pltpu.VMEM(scen_inverse.shape, BF16),
            pltpu.VMEM(scen_rhs.shape, BF16),
            pltpu.VMEM(first_block.shape, F32),
            pltpu.SemaphoreType.DMA((3,)),
            pltpu.SemaphoreType.DMA((capacity,)),
        ],
        compiler_params=pltpu.CompilerParams(vmem_limit_bytes=48 * 1024 * 1024),
        name="schur_terms",
    )(
        live_slots, place, in_hbm(link_mask), in_hbm(scen_inverse), link_border, in_hbm(scen_rhs), in_hbm(first_block),
        first_rhs[None, :],
    )
    own, other = sum_over_devices(keep, send)
    step = first_solve(blocks, lax.rem(place[1:2], 2), own, other)
    return pl.pallas_call(
        finish_kernel,
        grid=(capacity,),
        in_specs=[smem, whole(SUBLANES, link_width), per_slot(link_width, scen_width), per_slot(1, scen_width)],
        out_specs=[whole(link_width), whole(capacity, scen_width)],
        out_shape=[
            jax.ShapeDtypeStruct((link_width,), F32),
            jax.ShapeDtypeStruct((capacity, scen_width), F32),
        ],
        compiler_params=pltpu.CompilerParams(vmem_limit_bytes=48 * 1024 * 1024),
        name="scen_steps",
    )(live_slots, step, product, reduced)


def solution(mesh):
    return jax.shard_map(
        local,
        mesh=mesh,
        in_specs=(
            P(("scen", "section"), None, None),
            P(("scen", "section"), None, None),
            P(("scen", "section"), None),
            P(("scen", "section"), None),
            P(("scen", "section")),
            P("scen", "section"),
            P(),
        ),
        out_specs=(P(), P(("scen", "section"), None)),
        check_vma=False,
    )
```

```python
import functools

import jax
import jax.numpy as jnp
from jax import lax
from jax.experimental import pallas as pl
from jax.experimental.pallas import tpu as pltpu
from jax.sharding import PartitionSpec as P

SIDE = 4
STRIP = 8
LANES = 128
SUBLANES = 8
F32 = jnp.float32
BF16 = jnp.bfloat16
ROWS_ALONE = (((1,), (1,)), ((), ()))


def halves(value):
    high = value.astype(BF16)
    return high, (value - high.astype(F32)).astype(BF16)


def dot(left, right):
    return jnp.dot(left, right, preferred_element_type=F32)


def dot_rows(left, right):
    return lax.dot_general(left, right, ROWS_ALONE, preferred_element_type=F32)


def mixed(left, right):
    left_high, left_low = halves(left)
    right_high, right_low = halves(right)
    return dot(
        jnp.concatenate([left_high, left_low, left_high], axis=1),
        jnp.concatenate([right_high, right_high, right_low], axis=0),
    )


def mixed_rows(left, right):
    left_high, left_low = halves(left)
    right_high, right_low = halves(right)
    return dot_rows(
        jnp.concatenate([left_high, left_low, left_high], axis=1),
        jnp.concatenate([right_high, right_high, right_low], axis=1),
    )


def panel_base(j, blocks):
    return LANES * (j * blocks - j * (j - 1) // 2)


def terms_kernel(
    blocks, live_ref, place_ref, mask_hbm, inverse_hbm, border_ref, right_hbm, corner_hbm, first_ref,
    keep_ref, send_ref, product_ref, reduced_ref, total_ref, rows_ref, corner_wide_ref, rhs_ref,
    mask_ref, inverse_ref, right_ref, corner_ref, small_sems, inverse_sems,
):
    slot = pl.program_id(0)
    width = blocks * LANES
    corner_rows, corner_cols = corner_ref.shape
    small = [
        pltpu.make_async_copy(source, target, small_sems.at[i])
        for i, (source, target) in enumerate(
            ((mask_hbm, mask_ref), (right_hbm, right_ref), (corner_hbm, corner_ref))
        )
    ]

    def fetch(at):
        return pltpu.make_async_copy(inverse_hbm.at[at], inverse_ref.at[at], inverse_sems.at[at])

    @pl.when(slot == 0)
    def start():
        for at in range(inverse_ref.shape[0]):
            fetch(at).start()
        for copy in small:
            copy.start()
        total_ref[...] = jnp.zeros_like(total_ref)
        corner_wide_ref[...] = jnp.zeros_like(corner_wide_ref)
        for copy in small:
            copy.wait()
        corner_wide_ref[0:corner_rows, 0:corner_cols] = corner_ref[...]
        row_start = place_ref[0] * corner_rows
        col_start = place_ref[1] * corner_cols
        row_base = row_start // SUBLANES * SUBLANES
        col_base = col_start // LANES * LANES
        moved = pltpu.roll(corner_wide_ref[...], col_start - col_base, 1)
        moved = pltpu.roll(moved, row_start - row_base, 0)
        total_ref[
            pl.ds(pl.multiple_of(row_base, SUBLANES), corner_wide_ref.shape[0]),
            pl.ds(pl.multiple_of(col_base, LANES), corner_wide_ref.shape[1]),
        ] = moved
        at_origin = jnp.logical_and(place_ref[0] == 0, place_ref[1] == 0)
        rhs_ref[...] = jnp.where(at_origin, first_ref[...][None, :], 0.0)

    fetch(slot).wait()

    @pl.when(slot < live_ref[0])
    def add():
        mask = mask_ref[...]
        mask = jnp.sum(jnp.where(lax.broadcasted_iota(jnp.int32, mask.shape, 0) == slot, mask, 0), axis=0, keepdims=True)
        for c in range(blocks):
            at = slice(c * LANES, (c + 1) * LANES)
            turned = border_ref[0, :, at].T
            rows_ref[at, :] = turned * mask[:, c : c + 1].astype(F32).astype(BF16)
        inverse = inverse_ref[slot]
        product = dot(rows_ref[...], inverse).astype(BF16)
        product_ref[0] = product
        right = right_ref[...].astype(F32)
        right = jnp.sum(jnp.where(lax.broadcasted_iota(jnp.int32, right.shape, 0) == slot, right, 0.0), axis=0, keepdims=True)
        right = jnp.broadcast_to(right, (16, right.shape[1])).astype(BF16)
        reduced = dot(right, inverse)[0:1]
        reduced_ref[0] = reduced
        first, rest = halves(reduced)
        rest_wide = reduced - first.astype(F32)
        second, third = halves(rest_wide)
        row = lax.broadcasted_iota(jnp.int32, (16, reduced.shape[1]), 0)
        pieces = jnp.where(
            row == 0, first.astype(F32), jnp.where(row == 1, second.astype(F32), jnp.where(row == 2, third.astype(F32), 0.0))
        ).astype(BF16)
        rhs_ref[...] += jnp.sum(dot_rows(pieces, rows_ref[...]), axis=0, keepdims=True)
        for c in range(0, width, 2 * LANES):
            end = min(c + 2 * LANES, width)
            total_ref[c:width, c:end] += dot_rows(rows_ref[c:width, :], product[c:end, :])

    @pl.when(slot == pl.num_programs(0) - 1)
    def finish():
        cut = LANES // 2
        right_half = lax.broadcasted_iota(jnp.int32, (1, LANES), 1) >= cut
        places = [(j, i) for j in range(blocks) for i in range(j, blocks)]
        count = len(places) // 2

        def write(out_ref, own_places):
            for at, (j, i) in enumerate(own_places):
                base = at * LANES
                out_ref[base : base + LANES, :] = total_ref[i * LANES : (i + 1) * LANES, j * LANES : (j + 1) * LANES]
                if i == j:
                    own = rhs_ref[:, j * LANES : (j + 1) * LANES]
                    for row, value in ((0, own), (cut - 1, pltpu.roll(own, cut, 1))):
                        line = slice(base + row, base + row + 1)
                        out_ref[line, :] = jnp.where(right_half, value, out_ref[line, :])

        for core in range(2):

            @pl.when(lax.rem(place_ref[1], 2) == core)
            def write_both():
                write(keep_ref, places[core * count : (core + 1) * count])
                write(send_ref, places[(1 - core) * count : (2 - core) * count])


def invert(rows):
    count = len(rows)
    shape = (SUBLANES, LANES)
    lane = lax.broadcasted_iota(jnp.int32, shape, 1)
    sublane = lax.broadcasted_iota(jnp.int32, shape, 0)

    def across(block, c):
        return jnp.broadcast_to(block[:, c : c + 1], shape)

    def down(block, k):
        return jnp.broadcast_to(block[k : k + 1, :], shape)

    for p in range(count):
        at = p * SUBLANES
        strip = range(p // STRIP * STRIP, (p // STRIP + 1) * STRIP)
        carried = p + 1 in strip
        if p == strip[0]:
            own_columns = [across(rows[p], at + k) for k in range(SUBLANES)]
        inside = jnp.logical_and(lane >= at, lane < at + SUBLANES)
        own = jnp.where(inside, jnp.where(lane - at == sublane, 1.0, 0.0), rows[p])
        columns = [own_columns]
        following = []
        if carried:
            following = [across(rows[p + 1], at + k) for k in range(SUBLANES)]
            columns[0] = columns[0] + [across(rows[p], at + SUBLANES + k) for k in range(SUBLANES)]
            columns.append(following + [across(rows[p + 1], at + SUBLANES + k) for k in range(SUBLANES)])
        same = jnp.zeros(shape, F32)
        cross = jnp.zeros(shape, F32)
        for k in range(0, SUBLANES, 2):
            one, two = columns[0][k], columns[0][k + 1]
            a, b, c = down(one, k), down(two, k), down(two, k + 1)
            det = a * c - b * b
            rough = pl.reciprocal(det, approx=True)
            mend = 2.0 - det * rough
            free = jnp.logical_or(sublane < k, sublane > k + 1)
            factors = []
            for half, group in enumerate(columns):
                u, v = group[k], group[k + 1]
                first, second = ((u * c - v * b) * rough) * mend, ((v * a - u * b) * rough) * mend
                if half == 0:
                    first, second = jnp.where(free, first, 0.0), jnp.where(free, second, 0.0)
                factors.append((first, second))
            for m in range(k + 2, len(columns[0])):
                top, bottom = down(columns[0][m], k), down(columns[0][m], k + 1)
                for group, (first, second) in zip(columns, factors):
                    group[m] = (group[m] - first * top) - second * bottom
            first, second = factors[0]
            own = (own - first * down(own, k)) - second * down(own, k + 1)
            inverse = rough * mend
            same = jnp.where(sublane == k, c * inverse, jnp.where(sublane == k + 1, a * inverse, same))
            cross = jnp.where(free, cross, b * inverse)
        above, below = pltpu.roll(own, 1, 0), pltpu.roll(own, SUBLANES - 1, 0)
        own = same * own - cross * jnp.where(lax.rem(sublane, 2) == 0, below, above)
        spread = [down(own, k) for k in range(SUBLANES)]
        for v in [*range(p + 1, strip[-1] + 1), *range(strip[0], p)]:
            block = rows[v]
            spans = following if v == p + 1 else [across(block, at + k) for k in range(SUBLANES)]
            terms = [spans[k] * spread[k] for k in range(SUBLANES)]
            while len(terms) > 1:
                terms = [x + y for x, y in zip(terms[0::2], terms[1::2])]
            rows[v] = jnp.where(inside, 0.0, block) - terms[0]
        rows[p] = own
        if carried:
            own_columns = columns[1][SUBLANES:]
            continue
        others = [v % count for v in range(p + 1, p + 1 + count - STRIP)]
        rest = jnp.concatenate([rows[v] for v in others], axis=0)
        lane_wide = lax.broadcasted_iota(jnp.int32, rest.shape, 1)
        inside = jnp.logical_and(lane_wide >= strip[0] * SUBLANES, lane_wide < (p + 1) * SUBLANES)
        blank = jnp.zeros(shape, F32)
        own_rows = jnp.concatenate([rows[v] if v in strip else blank for v in range(count)], axis=0)
        rest = jnp.where(inside, 0.0, rest) - mixed(jnp.where(inside, rest, 0.0), own_rows)
        for i, v in enumerate(others):
            rows[v] = rest[i * SUBLANES : (i + 1) * SUBLANES]
    return rows


def add_up(parts):
    total = parts[0]
    for i in range(1, parts.shape[0]):
        total = total + parts[i]
    return total


def scatter_sum(value, axis, groups):
    size = len(groups[0])
    parts = value.reshape(size, value.shape[0] // size, LANES)
    return add_up(lax.all_to_all(parts, axis, 0, 0, axis_index_groups=groups))


def exchange(value, axis, groups):
    parts = jnp.broadcast_to(value[None], (len(groups[0]),) + value.shape)
    return lax.all_to_all(parts, axis, 0, 0, axis_index_groups=groups)


def gather(value, axis, groups):
    return exchange(value, axis, groups).reshape(len(groups[0]) * value.shape[0], LANES)


def sum_over_devices(keep, send):
    scen, section = lax.axis_size("scen"), lax.axis_size("section")
    depth = scen // SIDE
    far = depth // SIDE
    both = ("scen", "section")

    def at(z, y, x, core):
        return (z * SIDE + y) * section + 2 * x + core

    side, pair = range(SIDE), range(2)
    first, second = [], []
    for core in range(2):

        def along(z, major, minor, core=core):
            x, y = (major, minor) if core == 0 else (minor, major)
            return at(z, y, x, core)

        first += [
            [along(z, i, 2 * high + low) for i in side for low in pair] for z in range(depth) for high in pair
        ]
        second += [
            [along(z * SIDE + near, i, 2 * high + low) for high in pair for near in side]
            for z in range(far) for i in side for low in pair
        ]
    far_zs = [[(i * SIDE + z) * SIDE + y for i in range(far)] for z in side for y in side]
    value = keep + lax.ppermute(send, "section", [(i, i ^ 1) for i in range(section)])
    value = scatter_sum(value, both, first)
    value = scatter_sum(value, both, second)
    value = add_up(exchange(value, "scen", far_zs))
    value = gather(value, both, second)
    value = gather(value, both, first)
    return value, lax.ppermute(value, "section", [(i, i ^ 1) for i in range(section)])


def solve_kernel(blocks, core_ref, own_ref, other_ref, step_ref, work_ref, inverse_ref, turned_ref, rhs_ref, z_ref, x_ref):
    row = lax.broadcasted_iota(jnp.int32, (LANES, LANES), 0)
    column = lax.broadcasted_iota(jnp.int32, (LANES, LANES), 1)
    half = LANES // 2
    left_half = lax.broadcasted_iota(jnp.int32, (1, LANES), 1) < half
    scales, scale_columns = [], []
    height = own_ref.shape[0]

    def packed(base):
        at = slice(base % height, base % height + LANES)
        return jnp.where(core_ref[0] == base // height, own_ref[at, :], other_ref[at, :])

    for j in range(blocks):
        base = panel_base(j, blocks)
        square = packed(base)
        scale = lax.rsqrt(jnp.sum(jnp.where(row == column, square, 0.0), axis=0, keepdims=True))
        scales.append(scale)
        scale_columns.append(jnp.sum(jnp.where(row == column, scale, 0.0), axis=1, keepdims=True))
        moved = pltpu.roll(square[half - 1 : half, :], half, 1)
        own = jnp.where(left_half, moved, square[0:1, :]) * scale
        rhs_ref[j] = jnp.broadcast_to(own, (SUBLANES, LANES))
    for j in range(blocks):
        for i in range(j, blocks):
            base = panel_base(j, blocks) + (i - j) * LANES
            square = packed(base) * scale_columns[i] * scales[j]
            if i == j:
                square = jnp.where(row >= column, square, square.T)
            work_ref[base : base + LANES, :] = square

    def step(j, carry):
        base = pl.multiple_of(LANES * (j * blocks - lax.div(j * (j - 1), 2)), LANES)
        square = work_ref[pl.ds(base, LANES), :]
        rows = invert([square[v * SUBLANES : (v + 1) * SUBLANES] for v in range(LANES // SUBLANES)])
        inverse_ref[...] = jnp.concatenate(rows, axis=0)
        for jj in range(blocks):

            @pl.when(j == jj)
            def update():
                inverse = inverse_ref[...]
                at = panel_base(jj, blocks)
                rest = blocks - 1 - jj
                z = mixed(rhs_ref[jj], inverse)
                z_ref[jj] = z
                if rest == 0:
                    return
                panel_high, panel_low = halves(work_ref[at + LANES : at + (rest + 1) * LANES, :])
                high, low = halves(inverse)
                turned = dot(
                    jnp.concatenate([panel_high, panel_low, panel_high], axis=1),
                    jnp.concatenate([high, high, low], axis=0),
                )
                turned_ref[at + LANES : at + (rest + 1) * LANES, :] = turned
                high, low = halves(jnp.concatenate([turned, z, z], axis=0))
                left = jnp.concatenate([high, low, high], axis=1)
                right = jnp.concatenate([panel_high, panel_high, panel_low], axis=1)
                for s in range(0, rest, 2):
                    change = dot_rows(left[s * LANES :], right[s * LANES : min(s + 2, rest) * LANES])
                    for t in range(s, min(s + 2, rest)):
                        own = change[(t - s) * LANES :, (t - s) * LANES : (t - s + 1) * LANES]
                        height = (rest - t) * LANES
                        target = panel_base(jj + 1 + t, blocks)
                        work_ref[target : target + height, :] -= own[:height]
                        rhs_ref[jj + 1 + t] -= own[height : height + SUBLANES]

        return carry

    lax.fori_loop(0, blocks, step, 0)
    for j in reversed(range(blocks)):
        at = panel_base(j, blocks)
        rest = blocks - 1 - j
        x = z_ref[j]
        if rest:
            x = x - mixed(x_ref[:, (j + 1) * LANES :], turned_ref[at + LANES : at + (rest + 1) * LANES, :])
        x_ref[:, j * LANES : (j + 1) * LANES] = x
    for j in range(blocks):
        at = slice(j * LANES, (j + 1) * LANES)
        step_ref[:, at] = x_ref[:, at] * scales[j]


def first_solve(blocks, core, own, other):
    rows = panel_base(blocks, blocks)
    vmem = pl.BlockSpec(memory_space=pltpu.VMEM)
    square = (LANES, LANES)
    return pl.pallas_call(
        functools.partial(solve_kernel, blocks),
        in_specs=[pl.BlockSpec(memory_space=pltpu.SMEM), vmem, vmem],
        out_shape=jax.ShapeDtypeStruct((SUBLANES, blocks * LANES), F32),
        scratch_shapes=[
            pltpu.VMEM((rows, LANES), F32),
            pltpu.VMEM(square, F32),
            pltpu.VMEM((rows, LANES), F32),
            pltpu.VMEM((blocks, SUBLANES, LANES), F32),
            pltpu.VMEM((blocks, SUBLANES, LANES), F32),
            pltpu.VMEM((SUBLANES, blocks * LANES), F32),
        ],
        compiler_params=pltpu.CompilerParams(vmem_limit_bytes=48 * 1024 * 1024),
        name="first_solve",
    )(core, own, other)


def finish_kernel(live_ref, step_ref, product_ref, reduced_ref, first_ref, out_ref):
    slot = pl.program_id(0)
    first = step_ref[0:1, :]
    high, rest = halves(first)
    middle, low = halves(first - high.astype(F32))
    row = lax.broadcasted_iota(jnp.int32, (16, first.shape[1]), 0)
    pieces = jnp.where(
        row == 0, high.astype(F32), jnp.where(row == 1, middle.astype(F32), jnp.where(row == 2, low.astype(F32), 0.0))
    ).astype(BF16)
    moved = jnp.sum(dot(pieces, product_ref[0]), axis=0, keepdims=True)
    out_ref[pl.ds(slot, 1), :] = jnp.where(slot < live_ref[0], reduced_ref[0] - moved, 0.0)
    first_ref[...] = first[0]


def local(scen_inverse, link_border, scen_rhs, link_mask, live_slots, first_block, first_rhs):
    capacity, scen_width, link_width = link_border.shape
    blocks = link_width // LANES
    packed_rows = panel_base(blocks, blocks)
    place = jnp.stack([lax.axis_index("scen"), lax.axis_index("section")]).astype(jnp.int32)
    smem = pl.BlockSpec(memory_space=pltpu.SMEM)
    hbm = pl.BlockSpec(memory_space=pltpu.HBM)

    def in_hbm(value):
        return pltpu.with_memory_space_constraint(value, pltpu.HBM)

    def per_slot(*dims):
        return pl.BlockSpec((1,) + dims, lambda s: (s,) + (0,) * len(dims))

    def whole(*dims):
        return pl.BlockSpec(dims, lambda s: (0,) * len(dims))

    corner_height = -(-(first_block.shape[0] + SUBLANES - 1) // SUBLANES) * SUBLANES
    keep, send, product, reduced = pl.pallas_call(
        functools.partial(terms_kernel, blocks),
        grid=(capacity,),
        in_specs=[
            smem, smem, hbm, hbm,
            per_slot(scen_width, link_width),
            hbm, hbm,
            whole(link_width),
        ],
        out_specs=[
            whole(packed_rows // 2, LANES),
            whole(packed_rows // 2, LANES),
            per_slot(link_width, scen_width),
            per_slot(1, scen_width),
        ],
        out_shape=[
            jax.ShapeDtypeStruct((packed_rows // 2, LANES), F32),
            jax.ShapeDtypeStruct((packed_rows // 2, LANES), F32),
            jax.ShapeDtypeStruct((capacity, link_width, scen_width), BF16),
            jax.ShapeDtypeStruct((capacity, 1, scen_width), F32),
        ],
        scratch_shapes=[
            pltpu.VMEM((link_width + 2 * SUBLANES, link_width + LANES), F32),
            pltpu.VMEM((link_width, scen_width), BF16),
            pltpu.VMEM((corner_height, 2 * LANES), F32),
            pltpu.VMEM((1, link_width), F32),
            pltpu.VMEM(link_mask.shape, jnp.int32),
            pltpu.VMEM(scen_inverse.shape, BF16),
            pltpu.VMEM(scen_rhs.shape, BF16),
            pltpu.VMEM(first_block.shape, F32),
            pltpu.SemaphoreType.DMA((3,)),
            pltpu.SemaphoreType.DMA((capacity,)),
        ],
        compiler_params=pltpu.CompilerParams(vmem_limit_bytes=48 * 1024 * 1024),
        name="schur_terms",
    )(
        live_slots, place, in_hbm(link_mask), in_hbm(scen_inverse), link_border, in_hbm(scen_rhs), in_hbm(first_block),
        in_hbm(first_rhs),
    )
    own, other = sum_over_devices(keep, send)
    step = first_solve(blocks, lax.rem(place[1:2], 2), own, other)
    return pl.pallas_call(
        finish_kernel,
        grid=(capacity,),
        in_specs=[smem, whole(SUBLANES, link_width), per_slot(link_width, scen_width), per_slot(1, scen_width)],
        out_specs=[whole(link_width), whole(capacity, scen_width)],
        out_shape=[
            jax.ShapeDtypeStruct((link_width,), F32),
            jax.ShapeDtypeStruct((capacity, scen_width), F32),
        ],
        compiler_params=pltpu.CompilerParams(vmem_limit_bytes=48 * 1024 * 1024),
        name="scen_steps",
    )(live_slots, step, product, reduced)


def solution(mesh):
    return jax.shard_map(
        local,
        mesh=mesh,
        in_specs=(
            P(("scen", "section"), None, None),
            P(("scen", "section"), None, None),
            P(("scen", "section"), None),
            P(("scen", "section"), None),
            P(("scen", "section")),
            P("scen", "section"),
            P(),
        ),
        out_specs=(P(), P(("scen", "section"), None)),
        check_vma=False,
    )
```

```python
import functools

import jax
import jax.numpy as jnp
from jax import lax
from jax.experimental import pallas as pl
from jax.experimental.pallas import tpu as pltpu
from jax.sharding import PartitionSpec as P

SIDE = 4
STRIP = 4
LANES = 128
SUBLANES = 8
F32 = jnp.float32
BF16 = jnp.bfloat16
ROWS_ALONE = (((1,), (1,)), ((), ()))


def halves(value):
    high = value.astype(BF16)
    return high, (value - high.astype(F32)).astype(BF16)


def dot(left, right):
    return jnp.dot(left, right, preferred_element_type=F32)


def dot_rows(left, right):
    return lax.dot_general(left, right, ROWS_ALONE, preferred_element_type=F32)


def mixed(left, right):
    left_high, left_low = halves(left)
    right_high, right_low = halves(right)
    return dot(
        jnp.concatenate([left_high, left_low, left_high], axis=1),
        jnp.concatenate([right_high, right_high, right_low], axis=0),
    )


def mixed_rows(left, right):
    left_high, left_low = halves(left)
    right_high, right_low = halves(right)
    return dot_rows(
        jnp.concatenate([left_high, left_low, left_high], axis=1),
        jnp.concatenate([right_high, right_high, right_low], axis=1),
    )


def panel_base(j, blocks):
    return LANES * (j * blocks - j * (j - 1) // 2)


def terms_kernel(
    blocks, live_ref, place_ref, mask_hbm, inverse_hbm, border_ref, right_hbm, corner_hbm, first_ref,
    keep_ref, send_ref, product_ref, reduced_ref, total_ref, rows_ref, corner_wide_ref, rhs_ref,
    mask_ref, inverse_ref, right_ref, corner_ref, small_sems, inverse_sems,
):
    slot = pl.program_id(0)
    width = blocks * LANES
    corner_rows, corner_cols = corner_ref.shape
    small = [
        pltpu.make_async_copy(source, target, small_sems.at[i])
        for i, (source, target) in enumerate(
            ((mask_hbm, mask_ref), (right_hbm, right_ref), (corner_hbm, corner_ref))
        )
    ]

    def fetch(at):
        return pltpu.make_async_copy(inverse_hbm.at[at], inverse_ref.at[at], inverse_sems.at[at])

    @pl.when(slot == 0)
    def start():
        for at in range(inverse_ref.shape[0]):
            fetch(at).start()
        for copy in small:
            copy.start()
        total_ref[...] = jnp.zeros_like(total_ref)
        corner_wide_ref[...] = jnp.zeros_like(corner_wide_ref)
        for copy in small:
            copy.wait()
        corner_wide_ref[0:corner_rows, 0:corner_cols] = corner_ref[...]
        row_start = place_ref[0] * corner_rows
        col_start = place_ref[1] * corner_cols
        row_base = row_start // SUBLANES * SUBLANES
        col_base = col_start // LANES * LANES
        moved = pltpu.roll(corner_wide_ref[...], col_start - col_base, 1)
        moved = pltpu.roll(moved, row_start - row_base, 0)
        total_ref[
            pl.ds(pl.multiple_of(row_base, SUBLANES), corner_wide_ref.shape[0]),
            pl.ds(pl.multiple_of(col_base, LANES), corner_wide_ref.shape[1]),
        ] = moved
        at_origin = jnp.logical_and(place_ref[0] == 0, place_ref[1] == 0)
        rhs_ref[...] = jnp.where(at_origin, first_ref[...][None, :], 0.0)

    fetch(slot).wait()

    @pl.when(slot < live_ref[0])
    def add():
        mask = mask_ref[...]
        mask = jnp.sum(jnp.where(lax.broadcasted_iota(jnp.int32, mask.shape, 0) == slot, mask, 0), axis=0, keepdims=True)
        for c in range(blocks):
            at = slice(c * LANES, (c + 1) * LANES)
            turned = border_ref[0, :, at].T
            rows_ref[at, :] = turned * mask[:, c : c + 1].astype(F32).astype(BF16)
        inverse = inverse_ref[slot]
        product = dot(rows_ref[...], inverse).astype(BF16)
        product_ref[0] = product
        right = right_ref[...].astype(F32)
        right = jnp.sum(jnp.where(lax.broadcasted_iota(jnp.int32, right.shape, 0) == slot, right, 0.0), axis=0, keepdims=True)
        right = jnp.broadcast_to(right, (16, right.shape[1])).astype(BF16)
        reduced = dot(right, inverse)[0:1]
        reduced_ref[0] = reduced
        first, rest = halves(reduced)
        rest_wide = reduced - first.astype(F32)
        second, third = halves(rest_wide)
        row = lax.broadcasted_iota(jnp.int32, (16, reduced.shape[1]), 0)
        pieces = jnp.where(
            row == 0, first.astype(F32), jnp.where(row == 1, second.astype(F32), jnp.where(row == 2, third.astype(F32), 0.0))
        ).astype(BF16)
        rhs_ref[...] += jnp.sum(dot_rows(pieces, rows_ref[...]), axis=0, keepdims=True)
        for c in range(0, width, 2 * LANES):
            end = min(c + 2 * LANES, width)
            total_ref[c:width, c:end] += dot_rows(rows_ref[c:width, :], product[c:end, :])

    @pl.when(slot == pl.num_programs(0) - 1)
    def finish():
        cut = LANES // 2
        right_half = lax.broadcasted_iota(jnp.int32, (1, LANES), 1) >= cut
        places = [(j, i) for j in range(blocks) for i in range(j, blocks)]
        count = len(places) // 2

        def write(out_ref, own_places):
            for at, (j, i) in enumerate(own_places):
                base = at * LANES
                out_ref[base : base + LANES, :] = total_ref[i * LANES : (i + 1) * LANES, j * LANES : (j + 1) * LANES]
                if i == j:
                    own = rhs_ref[:, j * LANES : (j + 1) * LANES]
                    for row, value in ((0, own), (cut - 1, pltpu.roll(own, cut, 1))):
                        line = slice(base + row, base + row + 1)
                        out_ref[line, :] = jnp.where(right_half, value, out_ref[line, :])

        for core in range(2):

            @pl.when(lax.rem(place_ref[1], 2) == core)
            def write_both():
                write(keep_ref, places[core * count : (core + 1) * count])
                write(send_ref, places[(1 - core) * count : (2 - core) * count])


def invert(rows):
    count = len(rows)
    shape = (SUBLANES, LANES)
    lane = lax.broadcasted_iota(jnp.int32, shape, 1)
    sublane = lax.broadcasted_iota(jnp.int32, shape, 0)

    def across(block, c):
        return jnp.broadcast_to(block[:, c : c + 1], shape)

    def down(block, k):
        return jnp.broadcast_to(block[k : k + 1, :], shape)

    for p in range(count):
        at = p * SUBLANES
        strip = range(p // STRIP * STRIP, (p // STRIP + 1) * STRIP)
        carried = p + 1 in strip
        if p == strip[0]:
            own_columns = [across(rows[p], at + k) for k in range(SUBLANES)]
        inside = jnp.logical_and(lane >= at, lane < at + SUBLANES)
        own = jnp.where(inside, jnp.where(lane - at == sublane, 1.0, 0.0), rows[p])
        columns = [own_columns]
        following = []
        if carried:
            following = [across(rows[p + 1], at + k) for k in range(SUBLANES)]
            columns[0] = columns[0] + [across(rows[p], at + SUBLANES + k) for k in range(SUBLANES)]
            columns.append(following + [across(rows[p + 1], at + SUBLANES + k) for k in range(SUBLANES)])
        same = jnp.zeros(shape, F32)
        cross = jnp.zeros(shape, F32)
        for k in range(0, SUBLANES, 2):
            one, two = columns[0][k], columns[0][k + 1]
            a, b, c = down(one, k), down(two, k), down(two, k + 1)
            det = a * c - b * b
            rough = pl.reciprocal(det, approx=True)
            mend = 2.0 - det * rough
            free = jnp.logical_or(sublane < k, sublane > k + 1)
            factors = []
            for half, group in enumerate(columns):
                u, v = group[k], group[k + 1]
                first, second = ((u * c - v * b) * rough) * mend, ((v * a - u * b) * rough) * mend
                if half == 0:
                    first, second = jnp.where(free, first, 0.0), jnp.where(free, second, 0.0)
                factors.append((first, second))
            for m in range(k + 2, len(columns[0])):
                top, bottom = down(columns[0][m], k), down(columns[0][m], k + 1)
                for group, (first, second) in zip(columns, factors):
                    group[m] = (group[m] - first * top) - second * bottom
            first, second = factors[0]
            own = (own - first * down(own, k)) - second * down(own, k + 1)
            inverse = rough * mend
            same = jnp.where(sublane == k, c * inverse, jnp.where(sublane == k + 1, a * inverse, same))
            cross = jnp.where(free, cross, b * inverse)
        above, below = pltpu.roll(own, 1, 0), pltpu.roll(own, SUBLANES - 1, 0)
        own = same * own - cross * jnp.where(lax.rem(sublane, 2) == 0, below, above)
        spread = [down(own, k) for k in range(SUBLANES)]
        for v in [*range(p + 1, strip[-1] + 1), *range(strip[0], p)]:
            block = rows[v]
            spans = following if v == p + 1 else [across(block, at + k) for k in range(SUBLANES)]
            terms = [spans[k] * spread[k] for k in range(SUBLANES)]
            while len(terms) > 1:
                terms = [x + y for x, y in zip(terms[0::2], terms[1::2])]
            rows[v] = jnp.where(inside, 0.0, block) - terms[0]
        rows[p] = own
        if carried:
            own_columns = columns[1][SUBLANES:]
            continue
        others = [v % count for v in range(p + 1, p + 1 + count - STRIP)]
        rest = jnp.concatenate([rows[v] for v in others], axis=0)
        lane_wide = lax.broadcasted_iota(jnp.int32, rest.shape, 1)
        inside = jnp.logical_and(lane_wide >= strip[0] * SUBLANES, lane_wide < (p + 1) * SUBLANES)
        blank = jnp.zeros(shape, F32)
        own_rows = jnp.concatenate([rows[v] if v in strip else blank for v in range(count)], axis=0)
        rest = jnp.where(inside, 0.0, rest) - mixed(jnp.where(inside, rest, 0.0), own_rows)
        for i, v in enumerate(others):
            rows[v] = rest[i * SUBLANES : (i + 1) * SUBLANES]
    return rows


def add_up(parts):
    total = parts[0]
    for i in range(1, parts.shape[0]):
        total = total + parts[i]
    return total


def scatter_sum(value, axis, groups):
    size = len(groups[0])
    parts = value.reshape(size, value.shape[0] // size, LANES)
    return add_up(lax.all_to_all(parts, axis, 0, 0, axis_index_groups=groups))


def exchange(value, axis, groups):
    parts = jnp.broadcast_to(value[None], (len(groups[0]),) + value.shape)
    return lax.all_to_all(parts, axis, 0, 0, axis_index_groups=groups)


def gather(value, axis, groups):
    return exchange(value, axis, groups).reshape(len(groups[0]) * value.shape[0], LANES)


def sum_over_devices(keep, send):
    scen, section = lax.axis_size("scen"), lax.axis_size("section")
    depth = scen // SIDE
    far = depth // SIDE
    both = ("scen", "section")

    def at(z, y, x, core):
        return (z * SIDE + y) * section + 2 * x + core

    side, pair = range(SIDE), range(2)
    first, second = [], []
    for core in range(2):

        def along(z, major, minor, core=core):
            x, y = (major, minor) if core == 0 else (minor, major)
            return at(z, y, x, core)

        first += [
            [along(z, i, 2 * high + low) for i in side for low in pair] for z in range(depth) for high in pair
        ]
        second += [
            [along(z * SIDE + near, i, 2 * high + low) for high in pair for near in side]
            for z in range(far) for i in side for low in pair
        ]
    far_zs = [[(i * SIDE + z) * SIDE + y for i in range(far)] for z in side for y in side]
    value = keep + lax.ppermute(send, "section", [(i, i ^ 1) for i in range(section)])
    value = scatter_sum(value, both, first)
    value = scatter_sum(value, both, second)
    value = add_up(exchange(value, "scen", far_zs))
    value = gather(value, both, second)
    value = gather(value, both, first)
    return value, lax.ppermute(value, "section", [(i, i ^ 1) for i in range(section)])


def solve_kernel(blocks, core_ref, own_ref, other_ref, step_ref, work_ref, inverse_ref, turned_ref, rhs_ref, z_ref, x_ref):
    row = lax.broadcasted_iota(jnp.int32, (LANES, LANES), 0)
    column = lax.broadcasted_iota(jnp.int32, (LANES, LANES), 1)
    half = LANES // 2
    left_half = lax.broadcasted_iota(jnp.int32, (1, LANES), 1) < half
    scales, scale_columns = [], []
    height = own_ref.shape[0]

    def packed(base):
        at = slice(base % height, base % height + LANES)
        return jnp.where(core_ref[0] == base // height, own_ref[at, :], other_ref[at, :])

    for j in range(blocks):
        base = panel_base(j, blocks)
        square = packed(base)
        scale = lax.rsqrt(jnp.sum(jnp.where(row == column, square, 0.0), axis=0, keepdims=True))
        scales.append(scale)
        scale_columns.append(jnp.sum(jnp.where(row == column, scale, 0.0), axis=1, keepdims=True))
        moved = pltpu.roll(square[half - 1 : half, :], half, 1)
        own = jnp.where(left_half, moved, square[0:1, :]) * scale
        rhs_ref[j] = jnp.broadcast_to(own, (SUBLANES, LANES))
    for j in range(blocks):
        for i in range(j, blocks):
            base = panel_base(j, blocks) + (i - j) * LANES
            square = packed(base) * scale_columns[i] * scales[j]
            if i == j:
                square = jnp.where(row >= column, square, square.T)
            work_ref[base : base + LANES, :] = square

    def step(j, carry):
        base = pl.multiple_of(LANES * (j * blocks - lax.div(j * (j - 1), 2)), LANES)
        square = work_ref[pl.ds(base, LANES), :]
        rows = invert([square[v * SUBLANES : (v + 1) * SUBLANES] for v in range(LANES // SUBLANES)])
        inverse_ref[...] = jnp.concatenate(rows, axis=0)
        for jj in range(blocks):

            @pl.when(j == jj)
            def update():
                inverse = inverse_ref[...]
                at = panel_base(jj, blocks)
                rest = blocks - 1 - jj
                z = mixed(rhs_ref[jj], inverse)
                z_ref[jj] = z
                if rest == 0:
                    return
                panel_high, panel_low = halves(work_ref[at + LANES : at + (rest + 1) * LANES, :])
                high, low = halves(inverse)
                turned = dot(
                    jnp.concatenate([panel_high, panel_low, panel_high], axis=1),
                    jnp.concatenate([high, high, low], axis=0),
                )
                turned_ref[at + LANES : at + (rest + 1) * LANES, :] = turned
                high, low = halves(jnp.concatenate([turned, z, z], axis=0))
                left = jnp.concatenate([high, low, high], axis=1)
                right = jnp.concatenate([panel_high, panel_high, panel_low], axis=1)
                for s in range(0, rest, 2):
                    change = dot_rows(left[s * LANES :], right[s * LANES : min(s + 2, rest) * LANES])
                    for t in range(s, min(s + 2, rest)):
                        own = change[(t - s) * LANES :, (t - s) * LANES : (t - s + 1) * LANES]
                        height = (rest - t) * LANES
                        target = panel_base(jj + 1 + t, blocks)
                        work_ref[target : target + height, :] -= own[:height]
                        rhs_ref[jj + 1 + t] -= own[height : height + SUBLANES]

        return carry

    lax.fori_loop(0, blocks, step, 0)
    for j in reversed(range(blocks)):
        at = panel_base(j, blocks)
        rest = blocks - 1 - j
        x = z_ref[j]
        if rest:
            x = x - mixed(x_ref[:, (j + 1) * LANES :], turned_ref[at + LANES : at + (rest + 1) * LANES, :])
        x_ref[:, j * LANES : (j + 1) * LANES] = x
    for j in range(blocks):
        at = slice(j * LANES, (j + 1) * LANES)
        step_ref[:, at] = x_ref[:, at] * scales[j]


def first_solve(blocks, core, own, other):
    rows = panel_base(blocks, blocks)
    vmem = pl.BlockSpec(memory_space=pltpu.VMEM)
    square = (LANES, LANES)
    return pl.pallas_call(
        functools.partial(solve_kernel, blocks),
        in_specs=[pl.BlockSpec(memory_space=pltpu.SMEM), vmem, vmem],
        out_shape=jax.ShapeDtypeStruct((SUBLANES, blocks * LANES), F32),
        scratch_shapes=[
            pltpu.VMEM((rows, LANES), F32),
            pltpu.VMEM(square, F32),
            pltpu.VMEM((rows, LANES), F32),
            pltpu.VMEM((blocks, SUBLANES, LANES), F32),
            pltpu.VMEM((blocks, SUBLANES, LANES), F32),
            pltpu.VMEM((SUBLANES, blocks * LANES), F32),
        ],
        compiler_params=pltpu.CompilerParams(vmem_limit_bytes=48 * 1024 * 1024),
        name="first_solve",
    )(core, own, other)


def finish_kernel(live_ref, step_ref, product_ref, reduced_ref, first_ref, out_ref):
    slot = pl.program_id(0)
    first = step_ref[0:1, :]
    high, rest = halves(first)
    middle, low = halves(first - high.astype(F32))
    row = lax.broadcasted_iota(jnp.int32, (16, first.shape[1]), 0)
    pieces = jnp.where(
        row == 0, high.astype(F32), jnp.where(row == 1, middle.astype(F32), jnp.where(row == 2, low.astype(F32), 0.0))
    ).astype(BF16)
    moved = jnp.sum(dot(pieces, product_ref[0]), axis=0, keepdims=True)
    out_ref[pl.ds(slot, 1), :] = jnp.where(slot < live_ref[0], reduced_ref[0] - moved, 0.0)
    first_ref[...] = first[0]


def local(scen_inverse, link_border, scen_rhs, link_mask, live_slots, first_block, first_rhs):
    capacity, scen_width, link_width = link_border.shape
    blocks = link_width // LANES
    packed_rows = panel_base(blocks, blocks)
    place = jnp.stack([lax.axis_index("scen"), lax.axis_index("section")]).astype(jnp.int32)
    smem = pl.BlockSpec(memory_space=pltpu.SMEM)
    hbm = pl.BlockSpec(memory_space=pltpu.HBM)

    def in_hbm(value):
        return pltpu.with_memory_space_constraint(value, pltpu.HBM)

    def per_slot(*dims):
        return pl.BlockSpec((1,) + dims, lambda s: (s,) + (0,) * len(dims))

    def whole(*dims):
        return pl.BlockSpec(dims, lambda s: (0,) * len(dims))

    corner_height = -(-(first_block.shape[0] + SUBLANES - 1) // SUBLANES) * SUBLANES
    keep, send, product, reduced = pl.pallas_call(
        functools.partial(terms_kernel, blocks),
        grid=(capacity,),
        in_specs=[
            smem, smem, hbm, hbm,
            per_slot(scen_width, link_width),
            hbm, hbm,
            whole(link_width),
        ],
        out_specs=[
            whole(packed_rows // 2, LANES),
            whole(packed_rows // 2, LANES),
            per_slot(link_width, scen_width),
            per_slot(1, scen_width),
        ],
        out_shape=[
            jax.ShapeDtypeStruct((packed_rows // 2, LANES), F32),
            jax.ShapeDtypeStruct((packed_rows // 2, LANES), F32),
            jax.ShapeDtypeStruct((capacity, link_width, scen_width), BF16),
            jax.ShapeDtypeStruct((capacity, 1, scen_width), F32),
        ],
        scratch_shapes=[
            pltpu.VMEM((link_width + 2 * SUBLANES, link_width + LANES), F32),
            pltpu.VMEM((link_width, scen_width), BF16),
            pltpu.VMEM((corner_height, 2 * LANES), F32),
            pltpu.VMEM((1, link_width), F32),
            pltpu.VMEM(link_mask.shape, jnp.int32),
            pltpu.VMEM(scen_inverse.shape, BF16),
            pltpu.VMEM(scen_rhs.shape, BF16),
            pltpu.VMEM(first_block.shape, F32),
            pltpu.SemaphoreType.DMA((3,)),
            pltpu.SemaphoreType.DMA((capacity,)),
        ],
        compiler_params=pltpu.CompilerParams(vmem_limit_bytes=48 * 1024 * 1024),
        name="schur_terms",
    )(
        live_slots, place, in_hbm(link_mask), in_hbm(scen_inverse), link_border, in_hbm(scen_rhs), in_hbm(first_block),
        in_hbm(first_rhs),
    )
    own, other = sum_over_devices(keep, send)
    step = first_solve(blocks, lax.rem(place[1:2], 2), own, other)
    return pl.pallas_call(
        finish_kernel,
        grid=(capacity,),
        in_specs=[smem, whole(SUBLANES, link_width), per_slot(link_width, scen_width), per_slot(1, scen_width)],
        out_specs=[whole(link_width), whole(capacity, scen_width)],
        out_shape=[
            jax.ShapeDtypeStruct((link_width,), F32),
            jax.ShapeDtypeStruct((capacity, scen_width), F32),
        ],
        compiler_params=pltpu.CompilerParams(vmem_limit_bytes=48 * 1024 * 1024),
        name="scen_steps",
    )(live_slots, step, product, reduced)


def solution(mesh):
    return jax.shard_map(
        local,
        mesh=mesh,
        in_specs=(
            P(("scen", "section"), None, None),
            P(("scen", "section"), None, None),
            P(("scen", "section"), None),
            P(("scen", "section"), None),
            P(("scen", "section")),
            P("scen", "section"),
            P(),
        ),
        out_specs=(P(), P(("scen", "section"), None)),
        check_vma=False,
    )
```
